768 devices in a mesh: dp: 48 (over z, x_hi, core), aug: 16 (over x_lo, y).
Axes of the slice: x: 4 (x_hi: 2, x_lo: 2; x = x_hi * 2 + x_lo), y: 8, z: 12, core: 2. Of those that a mesh axis runs over, the one named last changes fastest.
Arguments:
- acts: bfloat16 [48, 16, 1664, 128], P('dp', 'aug'), may hold values from -6 to 6
- out_grads: bfloat16 [48, 16, 16, 312, 128], P('dp', 'aug'), may hold values from -60 to 60
- aug_count: int32 [48], P('dp'), may hold values from 4 to 16
- noise: float32 [4992, 1664], P('dp', 'aug'), may hold values from -6 to 6
- first_moment: float32 [4992, 1664], P('dp', 'aug'), may hold values from -6 to 6
- second_moment: float32 [4992, 1664], P('dp', 'aug'), may hold values from 0.1 to 4
Outputs:
- noisy_grad: float32 [4992, 1664], P('dp', 'aug')
- new_first: float32 [4992, 1664], P('dp', 'aug')
- new_second: float32 [4992, 1664], P('dp', 'aug')
The draws below stay inside these ranges and needn't reach their ends.
All inputs are finite; a program needn't handle non-finite values.
Results may differ from the reference program's by a relative error of at most 0.0003.
Values may be sent and summed in bfloat16 or wider, within the bound.
No kernel may reach another device: no remote copies, remote signals or barrier semaphores. Data moves between devices by JAX's collectives and lax.ppermute only.
A program may use at most 32 MiB of HBM per device.

```python
import math
import jax
import jax.numpy as jnp
from jax import lax

D = 1664
HEADS = 16
HS = 104
TOK = 128
IMAGES = 48
AUGS = 16


def draw_acts(key, part):
    key = jax.random.fold_in(key, 5)
    first, second, third = jax.random.split(key, 3)
    common = jax.random.normal(first, (1, 1, D, TOK), jnp.float32)
    image = jax.random.normal(second, (IMAGES, 1, D, TOK), jnp.float32)
    own = jax.random.normal(third, (IMAGES, AUGS, D, TOK), jnp.float32)
    mixed = 0.8 * common + 0.35 * image + 0.5 * own
    return jnp.clip(mixed, -6.0, 6.0).astype(jnp.bfloat16)


def draw_out_grads(key, part):
    key = jax.random.fold_in(key, 7)
    first, second, third, fourth = jax.random.split(key, 4)
    rest = (HEADS, 3 * HS, TOK)
    common = jax.random.normal(first, (1, 1) + rest, jnp.float32)
    image = jax.random.normal(second, (IMAGES, 1) + rest, jnp.float32)
    own = jax.random.normal(third, (IMAGES, AUGS) + rest, jnp.float32)
    base = 0.8 * common + 0.35 * image + 0.5 * own
    base = jnp.clip(base, -4.0, 4.0)
    image_scale = jnp.exp(jax.random.uniform(fourth, (IMAGES, 1, 1, 1, 1), jnp.float32, -3.5, 1.6))
    head_scale = (3.0 ** (jnp.arange(HEADS, dtype=jnp.float32) / (HEADS - 1))).reshape(1, 1, HEADS, 1, 1)
    return (base * image_scale * head_scale).astype(jnp.bfloat16)


def place_ends(entries, rng, low, top_value):
    extent = entries.shape
    spot = [jax.random.randint(jax.random.fold_in(rng, axis), (), 0, extent[axis]) for axis in range(len(extent))]
    entries = entries.at[tuple(spot)].set(low)
    longest = extent.index(max(extent))
    spot[longest] = (spot[longest] + 1) % extent[longest]
    return entries.at[tuple(spot)].set(top_value)


def levels(stream_key, shape, shards, smallest, largest):
    factor_of, own = 1.0, jax.random.fold_in(stream_key, 6)
    for position, parts in shards:
        draws = jnp.exp(jax.random.uniform(jax.random.fold_in(own, position), (parts,), jnp.float32, smallest / len(shards), largest / len(shards)))
        factor_of = factor_of * jnp.repeat(draws, shape[position] // parts).reshape([-1 if axis == position else 1 for axis in range(len(shape))])
    return factor_of


def normal_values(stream_key, extent, width, bound, cuts=(), kind=jnp.bfloat16):
    entries = width * jax.random.normal(stream_key, extent, jnp.float32)
    if cuts:
        entries = entries * levels(stream_key, extent, cuts, -0.22, 0.18)
    return jnp.clip(entries, -bound, bound).astype(kind)


def setup_inputs(seed: int = 0) -> dict:
    splits = jax.random.split(jax.random.key(seed), 7)
    return {
        "acts": draw_acts(jax.random.fold_in(splits[6], 71), 0),
        "out_grads": draw_out_grads(jax.random.fold_in(splits[6], 71), 0),
        "aug_count": place_ends(jax.random.randint(splits[2], (IMAGES,), max(1, AUGS // 4), AUGS + 1), jax.random.fold_in(splits[2], 1), max(1, AUGS // 4), AUGS).astype(jnp.int32),
        "noise": normal_values(splits[3], (3 * D, D), 1.0, 6.0, ((0, 48), (1, 16)), jnp.float32),
        "first_moment": normal_values(splits[4], (3 * D, D), 1.0, 6.0, ((0, 48), (1, 16)), jnp.float32),
        "second_moment": jnp.clip(jnp.exp(math.log(4.0) - 3.6888794 * jax.random.uniform(splits[5], (3 * D, D), jnp.float32) ** levels(splits[5], (3 * D, D), ((0, 48), (1, 16)), -0.2, 0.2)), 0.1, 4.0),
    }


def image_term(acts_one, grads_one, count, clip):
    live = (jnp.arange(AUGS) < count).astype(jnp.bfloat16)
    masked = grads_one * live[:, None, None, None]
    masked = masked.reshape(AUGS, HEADS, 3, HS, TOK).astype(jnp.float32)
    summed = jnp.einsum('aft,ahjet->jfhe', acts_one.astype(jnp.float32), masked, precision=lax.Precision.HIGHEST)
    summed = summed / count.astype(jnp.float32)
    norm = jnp.sqrt(jnp.sum(summed * summed) + 1e-06)
    factor = jnp.minimum(jnp.float32(1.0), clip / norm)
    return (factor * summed).reshape(3 * D, D)

def reference(acts, out_grads, aug_count, noise, first_moment, second_moment):
    clip = jnp.float32(0.5 * D * math.sqrt(3.0 * TOK / AUGS))
    sigma = jnp.float32(0.2 * math.sqrt(IMAGES) / D)

    def step(total, inputs):
        acts_one, grads_one, count = inputs
        return (total + image_term(acts_one, grads_one, count, clip), None)
    start = jnp.zeros((3 * D, D), jnp.float32)
    total, unused = lax.scan(step, start, (acts, out_grads, aug_count))
    noisy_grad = (total + sigma * clip * noise) / jnp.float32(IMAGES)
    new_first = 0.9 * first_moment + 0.1 * noisy_grad
    new_second = 0.999 * second_moment + 0.001 * noisy_grad * noisy_grad
    return (noisy_grad, new_first, new_second)
```

```python
import functools
import math

import jax
import jax.numpy as jnp
from jax import lax
from jax.experimental import pallas as pl
from jax.experimental.pallas import tpu as pltpu
from jax.sharding import Mesh
from jax.sharding import PartitionSpec as P

LANES = 128
TOP = 32767.0
VMEM = 48 * 1024 * 1024


def multiply_kernel(place, x_ref, own_ref, other_ref, keep_ref, send_ref, sum_ref, padded, squares, *, groups, span):
    step = pl.program_id(0)
    part, count = place[0], place[1]
    rings = x_ref.shape[0]
    size = own_ref.shape[2]
    tokens = x_ref.shape[3]

    @pl.when(step == 0)
    def _():
        padded[...] = jnp.zeros_like(padded)
        squares[...] = jnp.zeros_like(squares)
        for y in range(rings):
            for s in range(2):
                aug = jnp.bitwise_xor(part, s) * rings + y
                live = (aug < count).astype(jnp.float32).astype(jnp.bfloat16)
                for j in range(3):
                    for h, ref in enumerate((own_ref, other_ref)):
                        padded[y, j, h * LANES : h * LANES + size, s * tokens : (s + 1) * tokens] = ref[aug, j] * live

    scale = 1.0 / count.astype(jnp.float32)
    rows = x_ref.shape[2]
    blocks = rows // span
    both = jnp.where(part == 0, 1.0, 0.0)
    for j in range(3):
        acc = jnp.zeros((rows, 2 * LANES), jnp.float32)
        for y in range(rings):
            x = jnp.concatenate([x_ref[y, 0], x_ref[y, 1]], axis=1)
            acc += lax.dot_general(x, padded[y, j], (((1,), (1,)), ((), ())), preferred_element_type=jnp.float32)
        acc = (acc * scale).reshape(blocks, span, 2 * LANES)
        whole = acc[:, 8:] * acc[:, 8:]
        first = acc[:, :8] * acc[:, :8] * both
        total = jnp.sum(whole.reshape(blocks * (span // 8 - 1), 8, 2 * LANES), axis=0) + jnp.sum(first, axis=0)
        squares[...] += total[:, :LANES] + total[:, LANES:]

        @pl.when(step < groups)
        def _():
            for h in range(2):
                keep_ref[:, j, h] = acc[:, :, h * LANES : (h + 1) * LANES]

        @pl.when(step >= groups)
        def _():
            for h in range(2):
                send_ref[:, j, h] = acc[:, :, h * LANES : (h + 1) * LANES]

    sum_ref[...] = jnp.broadcast_to(jnp.sum(squares[...], keepdims=True), sum_ref.shape)


def clip_kernel(place, norms_ref, keep_ref, got_ref, out_ref, *, clip):
    part, core = place[0], place[1]
    half = norms_ref.shape[0] // 2
    factors = []
    for c in range(2):
        total = jnp.sum(norms_ref[c * half : (c + 1) * half], axis=0, keepdims=True)
        factors.append(jnp.minimum(1.0, clip / jnp.sqrt(total + 1e-06)))
    mine = jnp.where(core == 0, factors[0], factors[1])
    theirs = jnp.where(core == 0, factors[1], factors[0])
    lane = lax.broadcasted_iota(jnp.int32, keep_ref.shape[3:], 1)
    for j in range(3):
        for h in range(2):
            value = keep_ref[0, j, h] * mine + got_ref[0, j, h] * theirs
            top = jnp.maximum(jnp.max(jnp.abs(value), axis=1, keepdims=True), 1e-30)
            code = jnp.ceil(jnp.log2(top) * 8.0 + 0.05)
            value = jnp.round(value * (jnp.exp2(code * -0.125) * TOP))
            value = jnp.where(lane < 104, value, code)
            out_ref[j, 0, jnp.bitwise_xor(part, h)] = value.astype(jnp.int32).astype(jnp.int16)


def update_kernel(got_ref, noise_ref, first_ref, second_ref, grad_ref, new_first_ref, new_second_ref, *, weight, images):
    sums = []
    for part in range(2):
        total = jnp.zeros(got_ref.shape[2:], jnp.float32)
        for k in range(got_ref.shape[0]):
            value = got_ref[k, part].astype(jnp.int32).astype(jnp.float32)
            scale = jnp.exp2(value[:, 104:105] * 0.125) * (1.0 / TOP)
            total += value * scale
        sums.append(total)
    total = jnp.concatenate([sums[0], sums[1][8:]], axis=0)[:, :104]
    grad = (total + weight * noise_ref[...]) / images
    grad_ref[...] = grad
    new_first_ref[...] = 0.9 * first_ref[...] + 0.1 * grad
    new_second_ref[...] = 0.999 * second_ref[...] + 0.001 * grad * grad


def body(acts, out_grads, aug_count, noise, first_moment, second_moment):
    part, core = lax.axis_index("xl"), lax.axis_index("core")
    rings = lax.axis_size("y")
    augs = 2 * rings
    chips = lax.axis_size("z") * lax.axis_size("xh")
    images = 2 * chips
    width, tokens = acts.shape[2:]
    size = out_grads.shape[3] // 3
    clip = 0.5 * width * math.sqrt(3.0 * tokens / augs)
    sigma = 0.2 * math.sqrt(images) / width
    span = 56
    pairs = width // size // 2
    rows = pairs * 2 * span

    blocks = acts[0, 0].reshape(pairs, 2, size, tokens)

    def half_of(which):
        got = lax.dynamic_slice(blocks, (0, 0, which * (size - span), 0), (pairs, 2, span, tokens))
        mine = jnp.where(core == 0, got[:, 0], got[:, 1])
        sent = jnp.where(core == 0, got[:, 1], got[:, 0])
        return jnp.stack([mine, sent]).reshape(rows, tokens)

    swap = [(0, 1), (1, 0)]
    passed = lax.ppermute(half_of(1 - part), "xl", swap)
    x = lax.all_gather(jnp.stack([half_of(part), passed]), "y")

    own = lax.all_to_all(out_grads[0, 0], ("xl", "y"), 0, 0, tiled=True)
    other = lax.ppermute(own, "xl", swap)
    own = own.reshape(augs, 3, size, tokens)
    other = other.reshape(augs, 3, size, tokens)

    groups = 2
    tile = rows // (2 * groups)
    in_tile = tile // span
    whole = lambda *shape: pl.BlockSpec(shape, lambda i, place: (0,) * len(shape))
    keep, send, square = pl.pallas_call(
        functools.partial(multiply_kernel, groups=groups, span=span),
        grid_spec=pltpu.PrefetchScalarGridSpec(
            num_scalar_prefetch=1,
            grid=(2 * groups,),
            in_specs=[
                pl.BlockSpec((rings, 2, tile, tokens), lambda i, place: (0, 0, i, 0)),
                whole(augs, 3, size, tokens),
                whole(augs, 3, size, tokens),
            ],
            out_specs=[
                pl.BlockSpec((in_tile, 3, 2, span, LANES), lambda i, place: (jnp.minimum(i, groups - 1), 0, 0, 0, 0)),
                pl.BlockSpec((in_tile, 3, 2, span, LANES), lambda i, place: (jnp.maximum(i - groups, 0), 0, 0, 0, 0)),
                whole(8, LANES),
            ],
            scratch_shapes=[
                pltpu.VMEM((rings, 3, 2 * LANES, 2 * tokens), jnp.bfloat16),
                pltpu.VMEM((8, LANES), jnp.float32),
            ],
        ),
        out_shape=[
            jax.ShapeDtypeStruct((pairs, 3, 2, span, LANES), jnp.float32),
            jax.ShapeDtypeStruct((pairs, 3, 2, span, LANES), jnp.float32),
            jax.ShapeDtypeStruct((8, LANES), jnp.float32),
        ],
        compiler_params=pltpu.CompilerParams(vmem_limit_bytes=VMEM),
        name="multiply",
    )(jnp.stack([part, aug_count[0]]).astype(jnp.int32), x, own, other)

    got = lax.ppermute(send, "core", swap)
    group = 2 * augs
    norms = lax.all_to_all(jnp.broadcast_to(square[:1], (group, LANES)), ("core", "xl", "y"), 0, 0, tiled=True)

    pieces = pl.pallas_call(
        functools.partial(clip_kernel, clip=clip),
        grid_spec=pltpu.PrefetchScalarGridSpec(
            num_scalar_prefetch=1,
            grid=(pairs,),
            in_specs=[
                whole(group, LANES),
                pl.BlockSpec((1, 3, 2, span, LANES), lambda i, place: (i, 0, 0, 0, 0)),
                pl.BlockSpec((1, 3, 2, span, LANES), lambda i, place: (i, 0, 0, 0, 0)),
            ],
            out_specs=pl.BlockSpec((3, 1, 2, span, LANES), lambda i, place: (0, i, 0, 0, 0)),
        ),
        out_shape=jax.ShapeDtypeStruct((3, pairs, 2, span, LANES), jnp.int16),
        compiler_params=pltpu.CompilerParams(vmem_limit_bytes=VMEM),
        name="clip",
    )(jnp.stack([part, core]).astype(jnp.int32), norms, keep, got)

    pieces = pieces.reshape(2 * chips, span, LANES)
    pieces = lax.all_to_all(pieces, ("z", "xh", "xl"), 0, 0, tiled=True)
    state = jax.ShapeDtypeStruct(noise.shape, jnp.float32)
    return pl.pallas_call(
        functools.partial(update_kernel, weight=sigma * clip, images=float(images)),
        out_shape=[state, state, state],
        compiler_params=pltpu.CompilerParams(vmem_limit_bytes=VMEM),
        name="update",
    )(pieces.reshape(chips, 2, span, LANES), noise, first_moment, second_moment)


def solution(mesh):
    images, augs = mesh.devices.shape
    split = Mesh(mesh.devices.reshape(images // 4, 2, 2, 2, augs // 2), ("z", "xh", "core", "xl", "y"))
    dp, aug = ("z", "xh", "core"), ("xl", "y")
    state = P(dp, aug)
    run = jax.shard_map(
        body,
        mesh=split,
        in_specs=(P(dp, aug, None, None), P(dp, aug, None, None, None), P(dp), state, state, state),
        out_specs=(state, state, state),
        check_vma=False,
    )
    return lambda *args: tuple(run(*args))
```

```python
import functools
import math

import jax
import jax.numpy as jnp
from jax import lax
from jax.experimental import pallas as pl
from jax.experimental.pallas import tpu as pltpu
from jax.sharding import Mesh
from jax.sharding import PartitionSpec as P

LANES = 128
TOP = 32767.0
VMEM = 48 * 1024 * 1024
BIG, SMALL = 56, 48
SPARE = 24


def prepare_kernel(place, *refs):
    *ins, out_ref = refs
    part, count = place[0], place[1]
    half = len(ins) // 2
    rings = ins[0].shape[0] // 2
    size = ins[0].shape[2]
    out_ref[...] = jnp.zeros_like(out_ref)
    for y in range(rings):
        for s in range(2):
            aug = jnp.bitwise_xor(part, s) * rings + y
            live = (aug < count).astype(jnp.float32).astype(jnp.bfloat16)
            at = (2 * y + s) * LANES
            for h in range(2):
                j = 0
                for ref in ins[h * half : (h + 1) * half]:
                    for k in range(ref.shape[1]):
                        out_ref[j, at : at + LANES, h * LANES : h * LANES + size] = (ref[aug, k] * live).T
                        j += 1


def multiply_kernel(place, x_hbm, y_ref, out_ref, sum_ref, x_vmem, sems):
    part, core, count = place[0], place[1], place[2]
    slabs = x_hbm.shape[0]
    blocks = out_ref.shape[1] // 2
    tiles = []
    at = 0
    for span in (BIG, SMALL):
        for i in range(2):
            tiles.append((at, span, i * blocks))
            at += blocks * span
    copies = []
    for t, (row, span, _) in enumerate(tiles):
        rows = pl.ds(row, blocks * span)
        copies.append(pltpu.make_async_copy(x_hbm.at[:, rows], x_vmem.at[:, rows], sems.at[t]))
        copies[-1].start()
    scale = 1.0 / count.astype(jnp.float32)
    big_slot = (part != core).astype(jnp.int32)
    squares = jnp.zeros((8, LANES), jnp.float32)
    for t, (row, span, first) in enumerate(tiles):
        rows = blocks * span
        copies[t].wait()
        x = jnp.concatenate([x_vmem[k, row : row + rows] for k in range(slabs)], axis=1)
        slot = big_slot if span == BIG else 1 - big_slot
        for j in range(3):
            acc = jnp.dot(x, y_ref[j], preferred_element_type=jnp.float32) * scale
            square = jnp.sum((acc * acc).reshape(rows // 8, 8, 2 * LANES), axis=0)
            squares += square[:, :LANES] + square[:, LANES:]
            for b in range(blocks):
                for h in range(2):
                    out_ref[slot, first + b, j, h, :span] = acc[b * span : (b + 1) * span, h * LANES : (h + 1) * LANES]
                    if span < BIG:
                        out_ref[slot, first + b, j, h, span:] = jnp.zeros((BIG - span, LANES), jnp.float32)
    sum_ref[...] = jnp.broadcast_to(jnp.sum(squares, keepdims=True), sum_ref.shape)


def clip_kernel(place, norms_ref, keep_ref, got_ref, out_ref, *, clip, size):
    part, core = place[0], place[1]
    half = norms_ref.shape[0] // 2
    factors = []
    for c in range(2):
        total = jnp.sum(norms_ref[c * half : (c + 1) * half], axis=0, keepdims=True)
        factors.append(jnp.minimum(1.0, clip / jnp.sqrt(total + 1e-06)))
    mine = jnp.where(core == 0, factors[0], factors[1])
    theirs = jnp.where(core == 0, factors[1], factors[0])
    lane = lax.broadcasted_iota(jnp.int32, (8, LANES), 1)

    def block(k, carry):
        for j in range(3):
            for h in range(2):
                value = keep_ref[0, k, j, h] * mine + got_ref[0, k, j, h] * theirs
                top = jnp.maximum(jnp.max(jnp.abs(value), axis=1, keepdims=True), 1e-30)
                code = jnp.ceil(jnp.log2(top) * 8.0 + 0.05)
                value = jnp.round(value * (jnp.exp2(code * -0.125) * TOP))
                pieces = []
                for g in range(SMALL // 8):
                    if g < 5:
                        spare = pltpu.roll(value[SMALL:], (size - SPARE * g) % LANES, 1)
                    else:
                        spare = jnp.zeros((8, LANES), jnp.float32)
                        for q in range(BIG // 8):
                            spare = jnp.where(lane == size + q, code[8 * q : 8 * q + 8], spare)
                    pieces.append(jnp.where(lane < size, value[8 * g : 8 * g + 8], spare))
                piece = jnp.concatenate(pieces, axis=0)
                out_ref[j, k, jnp.bitwise_xor(part, h)] = piece.astype(jnp.int32).astype(jnp.int16)
        return carry

    lax.fori_loop(0, keep_ref.shape[1], block, 0)


def update_kernel(place, got_ref, noise_ref, first_ref, second_ref, grad_ref, new_first_ref, new_second_ref, *, weight, images):
    size = noise_ref.shape[1]
    lane = lax.broadcasted_iota(jnp.int32, (8, LANES), 1)
    zero = jnp.zeros((8, LANES), jnp.float32)
    halves = []
    for part in range(2):
        total = [zero] * (SMALL // 8)
        tails = [zero] * 5
        for k in range(got_ref.shape[0]):
            value = got_ref[k, part].astype(jnp.int32).astype(jnp.float32)
            scale = jnp.exp2(value[SMALL - 8 :] * 0.125) * (1.0 / TOP)
            for g in range(SMALL // 8):
                total[g] += value[8 * g : 8 * g + 8] * scale[:, size + g : size + g + 1]
            for g in range(5):
                tails[g] += value[8 * g : 8 * g + 8] * scale[:, size + 6 : size + 7]
        tail = zero
        for g in range(5):
            back = pltpu.roll(tails[g], (SPARE * g - size) % LANES, 1)
            tail = jnp.where((lane >= SPARE * g) & (lane < SPARE * (g + 1)), back, tail)
        halves.append(total + [tail])
    even = halves[0] + halves[1][:-1]
    odd = halves[0][:-1] + halves[1]
    total = jnp.concatenate([jnp.where(place[0] == 0, a, b) for a, b in zip(even, odd)], axis=0)[:, :size]
    grad = (total + weight * noise_ref[...]) / images
    grad_ref[...] = grad
    new_first_ref[...] = 0.9 * first_ref[...] + 0.1 * grad
    new_second_ref[...] = 0.999 * second_ref[...] + 0.001 * grad * grad


def call(kernel, out_shape, in_specs, **kw):
    return pl.pallas_call(
        kernel,
        in_specs=in_specs,
        out_shape=out_shape,
        compiler_params=pltpu.CompilerParams(vmem_limit_bytes=VMEM),
        **kw,
    )


def body(acts, out_grads, aug_count, noise, first_moment, second_moment):
    part, core = lax.axis_index("xl"), lax.axis_index("core")
    augs = 2 * lax.axis_size("y")
    chips = lax.axis_size("z") * lax.axis_size("xh")
    images = 2 * chips
    width, tokens = acts.shape[2:]
    size = out_grads.shape[3] // 3
    pairs = width // size // 2
    clip = 0.5 * width * math.sqrt(3.0 * tokens / augs)
    sigma = 0.2 * math.sqrt(images) / width
    smem = pl.BlockSpec(memory_space=pltpu.SMEM)
    vmem = pl.BlockSpec(memory_space=pltpu.VMEM)
    swap = [(0, 1), (1, 0)]

    blocks = acts[0, 0].reshape(pairs, 2, size, tokens)

    def half_of(which):
        big = lax.dynamic_slice(blocks, (0, which, (size - BIG) * which, 0), (pairs, 1, BIG, tokens))
        small = lax.dynamic_slice(blocks, (0, 1 - which, BIG * which, 0), (pairs, 1, SMALL, tokens))
        return jnp.concatenate([big.reshape(pairs * BIG, tokens), small.reshape(pairs * SMALL, tokens)])

    passed = lax.ppermute(half_of(1 - part), "xl", swap)
    x = lax.all_gather(jnp.stack([half_of(part), passed]), "y")
    x = x.reshape(augs, pairs * (BIG + SMALL), tokens)

    grads = out_grads[0, 0].reshape(augs, 3, size, tokens)
    own = [lax.all_to_all(g, ("xl", "y"), 0, 0, tiled=True) for g in (grads[:, :2], grads[:, 2:])]
    other = [lax.ppermute(g, "xl", swap) for g in own]
    y = call(
        prepare_kernel,
        jax.ShapeDtypeStruct((3, augs * tokens, 2 * LANES), jnp.bfloat16),
        [smem] + [vmem] * 4,
        name="prepare",
    )(jnp.stack([part, aug_count[0]]), *own, *other)

    group = 2 * augs
    share, square = call(
        multiply_kernel,
        [
            jax.ShapeDtypeStruct((2, pairs, 3, 2, BIG, LANES), jnp.float32),
            jax.ShapeDtypeStruct((group, LANES), jnp.float32),
        ],
        [smem, pl.BlockSpec(memory_space=pl.ANY), vmem],
        out_specs=[vmem, vmem],
        scratch_shapes=[pltpu.VMEM(x.shape, x.dtype), pltpu.SemaphoreType.DMA((4,))],
        name="multiply",
    )(jnp.stack([part, core, aug_count[0]]), x, y)

    norms = lax.all_to_all(square, ("core", "xl", "y"), 0, 0, tiled=True)
    got = lax.ppermute(share, "core", swap)
    half = (1, pairs, 3, 2, BIG, LANES)
    pieces = call(
        functools.partial(clip_kernel, clip=clip, size=size),
        jax.ShapeDtypeStruct((3, pairs, 2, SMALL, LANES), jnp.int16),
        [
            smem,
            pl.BlockSpec((group, LANES), lambda i: (0, 0)),
            pl.BlockSpec(half, lambda i: (0, 0, 0, 0, 0, 0)),
            pl.BlockSpec(half, lambda i: (1, 0, 0, 0, 0, 0)),
        ],
        grid=(1,),
        out_specs=pl.BlockSpec((3, pairs, 2, SMALL, LANES), lambda i: (0, 0, 0, 0, 0)),
        name="clip",
    )(jnp.stack([part, core]), norms, share, got)

    pieces = pieces.reshape(2 * chips, SMALL, LANES)
    pieces = lax.all_to_all(pieces, ("z", "xh", "xl"), 0, 0, tiled=True)
    state = jax.ShapeDtypeStruct(noise.shape, jnp.float32)
    return call(
        functools.partial(update_kernel, weight=sigma * clip, images=float(images)),
        [state, state, state],
        [smem] + [vmem] * 4,
        out_specs=[vmem] * 3,
        name="update",
    )(core.reshape(1), pieces.reshape(chips, 2, SMALL, LANES), noise, first_moment, second_moment)


def solution(mesh):
    images, augs = mesh.devices.shape
    split = Mesh(mesh.devices.reshape(images // 4, 2, 2, 2, augs // 2), ("z", "xh", "core", "xl", "y"))
    dp, aug = ("z", "xh", "core"), ("xl", "y")
    state = P(dp, aug)
    run = jax.shard_map(
        body,
        mesh=split,
        in_specs=(P(dp, aug, None, None), P(dp, aug, None, None, None), P(dp), state, state, state),
        out_specs=(state, state, state),
        check_vma=False,
    )
    return lambda *args: tuple(run(*args))
```

```python
import functools
import math

import jax
import jax.numpy as jnp
from jax import lax
from jax.experimental import pallas as pl
from jax.experimental.pallas import tpu as pltpu
from jax.sharding import Mesh
from jax.sharding import PartitionSpec as P

LANES = 128
TOP = 32767.0
VMEM = 48 * 1024 * 1024
BIG, SMALL = 56, 48
SPARE = 24


def stack_kernel(mine_ref, passed_ref, first_ref, out_ref):
    out_ref[0] = mine_ref[...]
    out_ref[1] = passed_ref[...]


def prepare_kernel(place, grads_hbm, *refs, shifts):
    *pieces, out_ref, held, sems = refs
    part, ring, count = place[0], place[1], place[2]
    rings = grads_hbm.shape[1]
    size = grads_hbm.shape[3]
    copies = [pltpu.make_async_copy(grads_hbm.at[:, ring], held.at[0], sems.at[0])]
    for i, piece in enumerate(pieces):
        copies.append(pltpu.make_async_copy(piece, held.at[i + 1], sems.at[i + 1]))
    for copy in copies:
        copy.start()
    for j in range(3):
        for h in range(2):
            out_ref[j, :, h * LANES + size : (h + 1) * LANES] = jnp.zeros((out_ref.shape[1], LANES - size), out_ref.dtype)
    for i, copy in enumerate(copies):
        copy.wait()
        y = lax.rem(ring - shifts[i % rings] + rings, rings)
        row = i // rings
        live = (jnp.bitwise_xor(part, row) * rings + y < count).astype(jnp.float32).astype(jnp.bfloat16)
        at = pl.multiple_of((2 * y + row) * LANES, LANES)
        for h in range(2):
            for j in range(3):
                out_ref[j, pl.ds(at, LANES), h * LANES : h * LANES + size] = (held[i, h, j] * live).T


def multiply_kernel(place, x_hbm, y_ref, out_hbm, sum_ref, x_vmem, out_ref, sems, out_sems):
    part, core, count = place[0], place[1], place[2]
    slabs = x_hbm.shape[0]
    blocks = out_ref.shape[1] // 2
    tiles = []
    at = 0
    for span in (BIG, SMALL):
        for i in range(2):
            tiles.append((at, span, i * blocks))
            at += blocks * span
    copies = []
    for t, (row, span, _) in enumerate(tiles):
        rows = pl.ds(row, blocks * span)
        copies.append(pltpu.make_async_copy(x_hbm.at[:, rows], x_vmem.at[:, rows], sems.at[t]))
        copies[-1].start()
    scale = 1.0 / count.astype(jnp.float32)
    big_slot = (part != core).astype(jnp.int32)
    squares = jnp.zeros((8, LANES), jnp.float32)
    for t, (row, span, first) in enumerate(tiles):
        rows = blocks * span
        copies[t].wait()
        x = jnp.concatenate([x_vmem[k, row : row + rows] for k in range(slabs)], axis=1)
        slot = big_slot if span == BIG else 1 - big_slot
        for j in range(3):
            acc = jnp.dot(x, y_ref[j], preferred_element_type=jnp.float32) * scale
            square = jnp.sum((acc * acc).reshape(rows // 8, 8, 2 * LANES), axis=0)
            squares += square[:, :LANES] + square[:, LANES:]
            for b in range(blocks):
                for h in range(2):
                    out_ref[slot, first + b, j, h, :span] = acc[b * span : (b + 1) * span, h * LANES : (h + 1) * LANES]
                    if span < BIG:
                        out_ref[slot, first + b, j, h, span:] = jnp.zeros((BIG - span, LANES), jnp.float32)
        some = pl.ds(first, blocks)
        copies.append(pltpu.make_async_copy(out_ref.at[slot, some], out_hbm.at[slot, some], out_sems.at[t]))
        copies[-1].start()
    sum_ref[...] = jnp.broadcast_to(jnp.sum(squares, keepdims=True), sum_ref.shape)
    for copy in copies[len(tiles) :]:
        copy.wait()


def clip_kernel(place, norms_ref, keep_ref, got_ref, out_ref, *, clip, size):
    core = place[0]
    half = norms_ref.shape[0] // 2
    factors = []
    for c in range(2):
        total = jnp.sum(norms_ref[c * half : (c + 1) * half], axis=0, keepdims=True)
        factors.append(jnp.minimum(1.0, clip / jnp.sqrt(total + 1e-06)))
    mine = jnp.where(core == 0, factors[0], factors[1])
    theirs = jnp.where(core == 0, factors[1], factors[0])
    lane = lax.broadcasted_iota(jnp.int32, (8, LANES), 1)

    def block(k, carry):
        for j in range(3):
            for h in range(2):
                value = keep_ref[0, k, j, h] * mine + got_ref[0, k, j, h] * theirs
                top = jnp.maximum(jnp.max(jnp.abs(value), axis=1, keepdims=True), 1e-30)
                code = jnp.ceil(jnp.log2(top) * 8.0 + 0.05)
                value = jnp.round(value * (jnp.exp2(code * -0.125) * TOP))
                pieces = []
                for g in range(SMALL // 8):
                    if g < 5:
                        spare = pltpu.roll(value[SMALL:], (size - SPARE * g) % LANES, 1)
                    else:
                        spare = jnp.zeros((8, LANES), jnp.float32)
                        for q in range(BIG // 8):
                            spare = jnp.where(lane == size + q, code[8 * q : 8 * q + 8], spare)
                    pieces.append(jnp.where(lane < size, value[8 * g : 8 * g + 8], spare))
                piece = jnp.concatenate(pieces, axis=0)
                out_ref[j, k, h] = piece.astype(jnp.int32).astype(jnp.int16)
        return carry

    lax.fori_loop(0, keep_ref.shape[1], block, 0)


def update_kernel(place, got_ref, noise_ref, first_ref, second_ref, grad_ref, new_first_ref, new_second_ref, *, weight, images):
    size = noise_ref.shape[1]
    lane = lax.broadcasted_iota(jnp.int32, (8, LANES), 1)
    zero = jnp.zeros((8, LANES), jnp.float32)
    halves = []
    for part in range(2):
        total = [zero] * (SMALL // 8)
        tails = [zero] * 5
        for k in range(got_ref.shape[0]):
            value = got_ref[k, part].astype(jnp.int32).astype(jnp.float32)
            scale = jnp.exp2(value[SMALL - 8 :] * 0.125) * (1.0 / TOP)
            for g in range(SMALL // 8):
                total[g] += value[8 * g : 8 * g + 8] * scale[:, size + g : size + g + 1]
            for g in range(5):
                tails[g] += value[8 * g : 8 * g + 8] * scale[:, size + 6 : size + 7]
        tail = zero
        for g in range(5):
            back = pltpu.roll(tails[g], (SPARE * g - size) % LANES, 1)
            tail = jnp.where((lane >= SPARE * g) & (lane < SPARE * (g + 1)), back, tail)
        halves.append(total + [tail])
    even = halves[0] + halves[1][:-1]
    odd = halves[0][:-1] + halves[1]
    total = jnp.concatenate([jnp.where(place[0] == 0, a, b) for a, b in zip(even, odd)], axis=0)[:, :size]
    grad = (total + weight * noise_ref[...]) / images
    grad_ref[...] = grad
    new_first_ref[...] = 0.9 * first_ref[...] + 0.1 * grad
    new_second_ref[...] = 0.999 * second_ref[...] + 0.001 * grad * grad


def call(kernel, out_shape, in_specs, **kw):
    return pl.pallas_call(
        kernel,
        in_specs=in_specs,
        out_shape=out_shape,
        compiler_params=pltpu.CompilerParams(vmem_limit_bytes=VMEM),
        **kw,
    )


def body(acts, out_grads, aug_count, noise, first_moment, second_moment):
    part, core, ring = lax.axis_index("xl"), lax.axis_index("core"), lax.axis_index("y")
    rings = lax.axis_size("y")
    augs = 2 * rings
    chips = lax.axis_size("z") * lax.axis_size("xh")
    images = 2 * chips
    width, tokens = acts.shape[2:]
    size = out_grads.shape[3] // 3
    pairs = width // size // 2
    clip = 0.5 * width * math.sqrt(3.0 * tokens / augs)
    sigma = 0.2 * math.sqrt(images) / width
    smem = pl.BlockSpec(memory_space=pltpu.SMEM)
    vmem = pl.BlockSpec(memory_space=pltpu.VMEM)
    swap = [(0, 1), (1, 0)]

    blocks = acts[0, 0].reshape(pairs, 2, size, tokens)

    def half_of(which):
        big = lax.dynamic_slice(blocks, (0, which, (size - BIG) * which, 0), (pairs, 1, BIG, tokens))
        small = lax.dynamic_slice(blocks, (0, 1 - which, BIG * which, 0), (pairs, 1, SMALL, tokens))
        return jnp.concatenate([big.reshape(pairs * BIG, tokens), small.reshape(pairs * SMALL, tokens)])

    passed = lax.ppermute(half_of(1 - part), "xl", swap)
    mine = half_of(part)

    grads = out_grads[0, 0].reshape(2, rings, 3, size, tokens)

    def shifted(shift):
        heads = lax.dynamic_index_in_dim(grads, lax.rem(ring + shift, rings), 1, keepdims=False)
        return lax.ppermute(heads, "y", [(i, (i + shift) % rings) for i in range(rings)]) if shift else heads

    shifts = (0, 4, 3, 5, 2, 6, 1, 7)
    pieces = [shifted(shift) for shift in shifts]
    stacked = call(
        stack_kernel,
        jax.ShapeDtypeStruct((2,) + mine.shape, mine.dtype),
        [vmem, vmem, pl.BlockSpec(memory_space=pl.ANY)],
        name="stack",
    )(mine, passed, pieces[1])
    x = lax.all_gather(stacked, "y")
    x = x.reshape(augs, pairs * (BIG + SMALL), tokens)
    pieces = pieces[1:] + [lax.ppermute(piece, "xl", swap) for piece in pieces]
    y = call(
        functools.partial(prepare_kernel, shifts=shifts),
        jax.ShapeDtypeStruct((3, augs * tokens, 2 * LANES), jnp.bfloat16),
        [smem] + [pl.BlockSpec(memory_space=pl.ANY)] * augs,
        scratch_shapes=[pltpu.VMEM((augs, 2, 3, size, tokens), jnp.bfloat16), pltpu.SemaphoreType.DMA((augs,))],
        name="prepare",
    )(jnp.stack([part, ring, aug_count[0]]), grads, *pieces)

    group = 2 * augs
    share, square = call(
        multiply_kernel,
        [
            jax.ShapeDtypeStruct((2, pairs, 3, 2, BIG, LANES), jnp.float32),
            jax.ShapeDtypeStruct((group, LANES), jnp.float32),
        ],
        [smem, pl.BlockSpec(memory_space=pl.ANY), vmem],
        out_specs=[pl.BlockSpec(memory_space=pl.ANY), vmem],
        scratch_shapes=[
            pltpu.VMEM(x.shape, x.dtype),
            pltpu.VMEM((2, pairs, 3, 2, BIG, LANES), jnp.float32),
            pltpu.SemaphoreType.DMA((4,)),
            pltpu.SemaphoreType.DMA((4,)),
        ],
        name="multiply",
    )(jnp.stack([part, core, aug_count[0]]), x, y)

    norms = lax.all_to_all(square, ("core", "xl", "y"), 0, 0, tiled=True)
    got = lax.ppermute(share, "core", swap)
    half = (1, pairs, 3, 2, BIG, LANES)
    pieces = call(
        functools.partial(clip_kernel, clip=clip, size=size),
        jax.ShapeDtypeStruct((3, pairs, 2, SMALL, LANES), jnp.int16),
        [
            smem,
            pl.BlockSpec((group, LANES), lambda i: (0, 0)),
            pl.BlockSpec(half, lambda i: (0, 0, 0, 0, 0, 0)),
            pl.BlockSpec(half, lambda i: (1, 0, 0, 0, 0, 0)),
        ],
        grid=(1,),
        out_specs=pl.BlockSpec((3, pairs, 2, SMALL, LANES), lambda i: (0, 0, 0, 0, 0)),
        name="clip",
    )(core.reshape(1), norms, share, got)

    pieces = pieces.reshape(2 * chips, SMALL, LANES)
    pieces = lax.all_to_all(pieces, ("z", "xh", "xl"), 0, 0, tiled=True)
    state = jax.ShapeDtypeStruct(noise.shape, jnp.float32)
    return call(
        functools.partial(update_kernel, weight=sigma * clip, images=float(images)),
        [state, state, state],
        [smem] + [vmem] * 4,
        out_specs=[vmem] * 3,
        name="update",
    )(core.reshape(1), pieces.reshape(chips, 2, SMALL, LANES), noise, first_moment, second_moment)


def solution(mesh):
    images, augs = mesh.devices.shape
    split = Mesh(mesh.devices.reshape(images // 4, 2, 2, 2, augs // 2), ("z", "xh", "core", "xl", "y"))
    dp, aug = ("z", "xh", "core"), ("xl", "y")
    state = P(dp, aug)
    run = jax.shard_map(
        body,
        mesh=split,
        in_specs=(P(dp, aug, None, None), P(dp, aug, None, None, None), P(dp), state, state, state),
        out_specs=(state, state, state),
        check_vma=False,
    )
    return lambda *args: tuple(run(*args))
```

```python
import functools
import math

import jax
import jax.numpy as jnp
from jax import lax
from jax.experimental import pallas as pl
from jax.experimental.pallas import tpu as pltpu
from jax.sharding import Mesh
from jax.sharding import PartitionSpec as P

LANES = 128
TOP = 32767.0
VMEM = 48 * 1024 * 1024
BIG, SMALL = 56, 48
SPARE = 24


def stack_kernel(mine_ref, passed_ref, near_ref, far_ref, out_ref):
    out_ref[0] = mine_ref[...]
    out_ref[1] = passed_ref[...]


def prepare_kernel(place, grads_ref, *refs, shifts):
    *pieces, out_ref = refs
    part, ring, count = place[0], place[1], place[2]
    rings = grads_ref.shape[1]
    size = grads_ref.shape[3]
    for j in range(3):
        for h in range(2):
            out_ref[j, :, h * LANES + size : (h + 1) * LANES] = jnp.zeros((out_ref.shape[1], LANES - size), out_ref.dtype)
    for i in range(2 * rings):
        y = lax.rem(ring - shifts[i % rings] + rings, rings)
        row = i // rings
        live = (jnp.bitwise_xor(part, row) * rings + y < count).astype(jnp.float32).astype(jnp.bfloat16)
        at = pl.multiple_of((2 * y + row) * LANES, LANES)
        for h in range(2):
            for j in range(3):
                value = pieces[i - 1][h, j] if i else grads_ref[h, ring, j]
                out_ref[j, pl.ds(at, LANES), h * LANES : h * LANES + size] = (value * live).T


def multiply_kernel(place, x_hbm, y_ref, out_ref, sum_ref, x_vmem, sems):
    part, core, count = place[0], place[1], place[2]
    slabs = x_hbm.shape[0]
    blocks = out_ref.shape[1] // 2
    tiles = []
    at = 0
    for span in (BIG, SMALL):
        for i in range(2):
            tiles.append((at, span, i * blocks))
            at += blocks * span
    copies = []
    for t, (row, span, _) in enumerate(tiles):
        rows = pl.ds(row, blocks * span)
        copies.append(pltpu.make_async_copy(x_hbm.at[:, rows], x_vmem.at[:, rows], sems.at[t]))
        copies[-1].start()
    scale = 1.0 / count.astype(jnp.float32)
    big_slot = (part != core).astype(jnp.int32)
    squares = jnp.zeros((8, LANES), jnp.float32)
    for t, (row, span, first) in enumerate(tiles):
        rows = blocks * span
        copies[t].wait()
        x = jnp.concatenate([x_vmem[k, row : row + rows] for k in range(slabs)], axis=1)
        slot = big_slot if span == BIG else 1 - big_slot
        for j in range(3):
            acc = jnp.dot(x, y_ref[j], preferred_element_type=jnp.float32) * scale
            square = jnp.sum((acc * acc).reshape(rows // 8, 8, 2 * LANES), axis=0)
            squares += square[:, :LANES] + square[:, LANES:]
            for b in range(blocks):
                for h in range(2):
                    out_ref[slot, first + b, j, h, :span] = acc[b * span : (b + 1) * span, h * LANES : (h + 1) * LANES]
                    if span < BIG:
                        out_ref[slot, first + b, j, h, span:] = jnp.zeros((BIG - span, LANES), jnp.float32)
    sum_ref[...] = jnp.broadcast_to(jnp.sum(squares, keepdims=True), sum_ref.shape)


def clip_kernel(place, norms_ref, keep_ref, got_ref, out_ref, *, clip, size):
    core = place[0]
    half = norms_ref.shape[0] // 2
    factors = []
    for c in range(2):
        total = jnp.sum(norms_ref[c * half : (c + 1) * half], axis=0, keepdims=True)
        factors.append(jnp.minimum(1.0, clip / jnp.sqrt(total + 1e-06)))
    mine = jnp.where(core == 0, factors[0], factors[1])
    theirs = jnp.where(core == 0, factors[1], factors[0])
    lane = lax.broadcasted_iota(jnp.int32, (8, LANES), 1)

    def block(k, carry):
        for j in range(3):
            for h in range(2):
                value = keep_ref[0, k, j, h] * mine + got_ref[0, k, j, h] * theirs
                top = jnp.maximum(jnp.max(jnp.abs(value), axis=1, keepdims=True), 1e-30)
                code = jnp.ceil(jnp.log2(top) * 8.0 + 0.05)
                value = jnp.round(value * (jnp.exp2(code * -0.125) * TOP))
                pieces = []
                for g in range(SMALL // 8):
                    if g < 5:
                        spare = pltpu.roll(value[SMALL:], (size - SPARE * g) % LANES, 1)
                    else:
                        spare = jnp.zeros((8, LANES), jnp.float32)
                        for q in range(BIG // 8):
                            spare = jnp.where(lane == size + q, code[8 * q : 8 * q + 8], spare)
                    pieces.append(jnp.where(lane < size, value[8 * g : 8 * g + 8], spare))
                piece = jnp.concatenate(pieces, axis=0)
                out_ref[j, k, h] = piece.astype(jnp.int32).astype(jnp.int16)
        return carry

    lax.fori_loop(0, keep_ref.shape[1], block, 0)


def update_kernel(place, got_ref, noise_ref, first_ref, second_ref, grad_ref, new_first_ref, new_second_ref, *, weight, images):
    size = noise_ref.shape[1]
    lane = lax.broadcasted_iota(jnp.int32, (8, LANES), 1)
    zero = jnp.zeros((8, LANES), jnp.float32)
    halves = []
    for part in range(2):
        total = [zero] * (SMALL // 8)
        tails = [zero] * 5
        for k in range(got_ref.shape[0]):
            value = got_ref[k, part].astype(jnp.int32).astype(jnp.float32)
            scale = jnp.exp2(value[SMALL - 8 :] * 0.125) * (1.0 / TOP)
            for g in range(SMALL // 8):
                total[g] += value[8 * g : 8 * g + 8] * scale[:, size + g : size + g + 1]
            for g in range(5):
                tails[g] += value[8 * g : 8 * g + 8] * scale[:, size + 6 : size + 7]
        tail = zero
        for g in range(5):
            back = pltpu.roll(tails[g], (SPARE * g - size) % LANES, 1)
            tail = jnp.where((lane >= SPARE * g) & (lane < SPARE * (g + 1)), back, tail)
        halves.append(total + [tail])
    even = halves[0] + halves[1][:-1]
    odd = halves[0][:-1] + halves[1]
    total = jnp.concatenate([jnp.where(place[0] == 0, a, b) for a, b in zip(even, odd)], axis=0)[:, :size]
    grad = (total + weight * noise_ref[...]) / images
    grad_ref[...] = grad
    new_first_ref[...] = 0.9 * first_ref[...] + 0.1 * grad
    new_second_ref[...] = 0.999 * second_ref[...] + 0.001 * grad * grad


def call(kernel, out_shape, in_specs, **kw):
    return pl.pallas_call(
        kernel,
        in_specs=in_specs,
        out_shape=out_shape,
        compiler_params=pltpu.CompilerParams(vmem_limit_bytes=VMEM),
        **kw,
    )


def body(acts, out_grads, aug_count, noise, first_moment, second_moment):
    part, core, ring = lax.axis_index("xl"), lax.axis_index("core"), lax.axis_index("y")
    rings = lax.axis_size("y")
    augs = 2 * rings
    chips = lax.axis_size("z") * lax.axis_size("xh")
    images = 2 * chips
    width, tokens = acts.shape[2:]
    size = out_grads.shape[3] // 3
    pairs = width // size // 2
    clip = 0.5 * width * math.sqrt(3.0 * tokens / augs)
    sigma = 0.2 * math.sqrt(images) / width
    smem = pl.BlockSpec(memory_space=pltpu.SMEM)
    vmem = pl.BlockSpec(memory_space=pltpu.VMEM)
    hbm = pl.BlockSpec(memory_space=pltpu.HBM)
    swap = [(0, 1), (1, 0)]

    blocks = acts[0, 0].reshape(pairs, 2, size, tokens)

    def half_of(which):
        big = lax.dynamic_slice(blocks, (0, which, (size - BIG) * which, 0), (pairs, 1, BIG, tokens))
        small = lax.dynamic_slice(blocks, (0, 1 - which, BIG * which, 0), (pairs, 1, SMALL, tokens))
        return jnp.concatenate([big.reshape(pairs * BIG, tokens), small.reshape(pairs * SMALL, tokens)])

    passed = lax.ppermute(half_of(1 - part), "xl", swap)
    mine = half_of(part)

    grads = out_grads[0, 0].reshape(2, rings, 3, size, tokens)

    def shifted(shift):
        heads = lax.dynamic_index_in_dim(grads, lax.rem(ring + shift, rings), 1, keepdims=False)
        return lax.ppermute(heads, "y", [(i, (i + shift) % rings) for i in range(rings)]) if shift else heads

    shifts = (0, 1, 7, 4, 3, 5, 2, 6)
    pieces = [shifted(shift) for shift in shifts]
    stacked = call(
        stack_kernel,
        jax.ShapeDtypeStruct((2,) + mine.shape, mine.dtype),
        [vmem, vmem, pl.BlockSpec(memory_space=pl.ANY), pl.BlockSpec(memory_space=pl.ANY)],
        name="stack",
    )(mine, passed, pieces[1], pieces[2])
    x = lax.all_gather(stacked, "y")
    x = x.reshape(augs, pairs * (BIG + SMALL), tokens)
    pieces = pieces[1:] + [lax.ppermute(piece, "xl", swap) for piece in pieces]
    y = call(
        functools.partial(prepare_kernel, shifts=shifts),
        jax.ShapeDtypeStruct((3, augs * tokens, 2 * LANES), jnp.bfloat16),
        [smem] + [vmem] * augs,
        name="prepare",
    )(jnp.stack([part, ring, aug_count[0]]), grads, *pieces)

    group = 2 * augs
    share, square = call(
        multiply_kernel,
        [
            jax.ShapeDtypeStruct((2, pairs, 3, 2, BIG, LANES), jnp.float32),
            jax.ShapeDtypeStruct((group, LANES), jnp.float32),
        ],
        [smem, hbm, vmem],
        out_specs=[vmem, vmem],
        scratch_shapes=[pltpu.VMEM(x.shape, x.dtype), pltpu.SemaphoreType.DMA((4,))],
        name="multiply",
    )(jnp.stack([part, core, aug_count[0]]), x, y)

    norms = lax.all_to_all(square, ("core", "xl", "y"), 0, 0, tiled=True)
    got = lax.ppermute(share, "core", swap)
    half = (1, pairs, 3, 2, BIG, LANES)
    pieces = call(
        functools.partial(clip_kernel, clip=clip, size=size),
        jax.ShapeDtypeStruct((3, pairs, 2, SMALL, LANES), jnp.int16),
        [
            smem,
            pl.BlockSpec((group, LANES), lambda i: (0, 0)),
            pl.BlockSpec(half, lambda i: (0, 0, 0, 0, 0, 0)),
            pl.BlockSpec(half, lambda i: (1, 0, 0, 0, 0, 0)),
        ],
        grid=(1,),
        out_specs=pl.BlockSpec((3, pairs, 2, SMALL, LANES), lambda i: (0, 0, 0, 0, 0)),
        name="clip",
    )(core.reshape(1), norms, share, got)

    pieces = pieces.reshape(2 * chips, SMALL, LANES)
    pieces = lax.all_to_all(pieces, ("z", "xh", "xl"), 0, 0, tiled=True)
    state = jax.ShapeDtypeStruct(noise.shape, jnp.float32)
    return call(
        functools.partial(update_kernel, weight=sigma * clip, images=float(images)),
        [state, state, state],
        [smem] + [vmem] * 4,
        out_specs=[vmem] * 3,
        name="update",
    )(core.reshape(1), pieces.reshape(chips, 2, SMALL, LANES), noise, first_moment, second_moment)


def solution(mesh):
    images, augs = mesh.devices.shape
    split = Mesh(mesh.devices.reshape(images // 4, 2, 2, 2, augs // 2), ("z", "xh", "core", "xl", "y"))
    dp, aug = ("z", "xh", "core"), ("xl", "y")
    state = P(dp, aug)
    run = jax.shard_map(
        body,
        mesh=split,
        in_specs=(P(dp, aug, None, None), P(dp, aug, None, None, None), P(dp), state, state, state),
        out_specs=(state, state, state),
        check_vma=False,
    )
    return lambda *args: tuple(run(*args))
```

```python
import functools
import math

import jax
import jax.numpy as jnp
from jax import lax
from jax.experimental import pallas as pl
from jax.experimental.pallas import tpu as pltpu
from jax.sharding import Mesh
from jax.sharding import PartitionSpec as P

LANES = 128
TOP = 32767.0
VMEM = 48 * 1024 * 1024
MOST_VMEM = 51200 * 1024
BIG, SMALL = 56, 48
SPARE = 24


def prepare_kernel(place, grads_ref, *refs, shifts):
    *pieces, out_ref = refs
    part, ring, count = place[0], place[1], place[2]
    rings = grads_ref.shape[1]
    size = grads_ref.shape[3]
    for j in range(3):
        for h in range(2):
            out_ref[j, :, h * LANES + size : (h + 1) * LANES] = jnp.zeros((out_ref.shape[1], LANES - size), out_ref.dtype)
    for i in range(2 * rings):
        y = lax.rem(ring - shifts[i % rings] + rings, rings)
        row = i // rings
        live = (jnp.bitwise_xor(part, row) * rings + y < count).astype(jnp.float32).astype(jnp.bfloat16)
        at = pl.multiple_of((2 * y + row) * LANES, LANES)
        for h in range(2):
            for j in range(3):
                value = pieces[i - 1][h, j] if i else grads_ref[h, ring, j]
                out_ref[j, pl.ds(at, LANES), h * LANES : h * LANES + size] = (value * live).T


def multiply_kernel(place, x_hbm, y_hbm, out_ref, sum_ref, x_vmem, y_vmem, sems, y_sems):
    part, core, count = place[0], place[1], place[2]
    slabs = x_hbm.shape[0]
    blocks = out_ref.shape[1] // 2
    tiles = []
    at = 0
    for span in (BIG, SMALL):
        for i in range(2):
            tiles.append((at, span, i * blocks))
            at += blocks * span
    copies = []
    for t, (row, span, _) in enumerate(tiles):
        rows = pl.ds(row, blocks * span)
        copies.append(pltpu.make_async_copy(x_hbm.at[:, rows], x_vmem.at[:, rows], sems.at[t]))
    y_copies = [pltpu.make_async_copy(y_hbm.at[j], y_vmem.at[j], y_sems.at[j]) for j in range(3)]
    copies[0].start()
    for copy in y_copies:
        copy.start()
    for copy in copies[1:]:
        copy.start()
    scale = 1.0 / count.astype(jnp.float32)
    big_slot = (part != core).astype(jnp.int32)
    squares = jnp.zeros((8, LANES), jnp.float32)
    for t, (row, span, first) in enumerate(tiles):
        rows = blocks * span
        copies[t].wait()
        x = jnp.concatenate([x_vmem[k, row : row + rows] for k in range(slabs)], axis=1)
        slot = big_slot if span == BIG else 1 - big_slot
        for j in range(3):
            if t == 0:
                y_copies[j].wait()
            acc = jnp.dot(x, y_vmem[j], preferred_element_type=jnp.float32) * scale
            square = jnp.sum((acc * acc).reshape(rows // 8, 8, 2 * LANES), axis=0)
            squares += square[:, :LANES] + square[:, LANES:]
            for b in range(blocks):
                for h in range(2):
                    out_ref[slot, first + b, j, h, :span] = acc[b * span : (b + 1) * span, h * LANES : (h + 1) * LANES]
                    if span < BIG:
                        out_ref[slot, first + b, j, h, span:] = jnp.zeros((BIG - span, LANES), jnp.float32)
    sum_ref[...] = jnp.broadcast_to(jnp.sum(squares, keepdims=True), sum_ref.shape)


def clip_kernel(place, norms_ref, keep_ref, got_ref, out_ref, *, clip, size):
    core = place[0]
    half = norms_ref.shape[0] // 2
    factors = []
    for c in range(2):
        total = jnp.sum(norms_ref[c * half : (c + 1) * half], axis=0, keepdims=True)
        factors.append(jnp.minimum(1.0, clip / jnp.sqrt(total + 1e-06)))
    mine = jnp.where(core == 0, factors[0], factors[1])
    theirs = jnp.where(core == 0, factors[1], factors[0])
    lane = lax.broadcasted_iota(jnp.int32, (8, LANES), 1)

    def block(k, carry):
        for j in range(3):
            for h in range(2):
                value = keep_ref[0, k, j, h] * mine + got_ref[0, k, j, h] * theirs
                top = jnp.maximum(jnp.max(jnp.abs(value), axis=1, keepdims=True), 1e-30)
                code = jnp.ceil(jnp.log2(top) * 8.0 + 0.05)
                value = jnp.round(value * (jnp.exp2(code * -0.125) * TOP))
                pieces = []
                for g in range(SMALL // 8):
                    if g < 5:
                        spare = pltpu.roll(value[SMALL:], (size - SPARE * g) % LANES, 1)
                    else:
                        spare = jnp.zeros((8, LANES), jnp.float32)
                        for q in range(BIG // 8):
                            spare = jnp.where(lane == size + q, code[8 * q : 8 * q + 8], spare)
                    pieces.append(jnp.where(lane < size, value[8 * g : 8 * g + 8], spare))
                piece = jnp.concatenate(pieces, axis=0)
                out_ref[j, k, h] = piece.astype(jnp.int32).astype(jnp.int16)
        return carry

    lax.fori_loop(0, keep_ref.shape[1], block, 0)


def update_kernel(place, got_ref, noise_ref, first_ref, second_ref, grad_ref, new_first_ref, new_second_ref, *, weight, images):
    size = noise_ref.shape[1]
    lane = lax.broadcasted_iota(jnp.int32, (8, LANES), 1)
    zero = jnp.zeros((8, LANES), jnp.float32)
    halves = []
    for part in range(2):
        total = [zero] * (SMALL // 8)
        tails = [zero] * 5
        for k in range(got_ref.shape[0]):
            value = got_ref[k, part].astype(jnp.int32).astype(jnp.float32)
            scale = jnp.exp2(value[SMALL - 8 :] * 0.125) * (1.0 / TOP)
            for g in range(SMALL // 8):
                total[g] += value[8 * g : 8 * g + 8] * scale[:, size + g : size + g + 1]
            for g in range(5):
                tails[g] += value[8 * g : 8 * g + 8] * scale[:, size + 6 : size + 7]
        tail = zero
        for g in range(5):
            back = pltpu.roll(tails[g], (SPARE * g - size) % LANES, 1)
            tail = jnp.where((lane >= SPARE * g) & (lane < SPARE * (g + 1)), back, tail)
        halves.append(total + [tail])
    even = halves[0] + halves[1][:-1]
    odd = halves[0][:-1] + halves[1]
    total = jnp.concatenate([jnp.where(place[0] == 0, a, b) for a, b in zip(even, odd)], axis=0)[:, :size]
    grad = (total + weight * noise_ref[...]) / images
    grad_ref[...] = grad
    new_first_ref[...] = 0.9 * first_ref[...] + 0.1 * grad
    new_second_ref[...] = 0.999 * second_ref[...] + 0.001 * grad * grad


def call(kernel, out_shape, in_specs, limit=VMEM, **kw):
    return pl.pallas_call(
        kernel,
        in_specs=in_specs,
        out_shape=out_shape,
        compiler_params=pltpu.CompilerParams(vmem_limit_bytes=limit),
        **kw,
    )


def body(acts, out_grads, aug_count, noise, first_moment, second_moment):
    part, core, ring = lax.axis_index("xl"), lax.axis_index("core"), lax.axis_index("y")
    rings = lax.axis_size("y")
    augs = 2 * rings
    chips = lax.axis_size("z") * lax.axis_size("xh")
    images = 2 * chips
    width, tokens = acts.shape[2:]
    size = out_grads.shape[3] // 3
    pairs = width // size // 2
    clip = 0.5 * width * math.sqrt(3.0 * tokens / augs)
    sigma = 0.2 * math.sqrt(images) / width
    smem = pl.BlockSpec(memory_space=pltpu.SMEM)
    vmem = pl.BlockSpec(memory_space=pltpu.VMEM)
    hbm = pl.BlockSpec(memory_space=pltpu.HBM)
    swap = [(0, 1), (1, 0)]

    blocks = acts[0, 0].reshape(pairs, 2, size, tokens)

    def half_of(which):
        big = lax.dynamic_slice(blocks, (0, which, (size - BIG) * which, 0), (pairs, 1, BIG, tokens))
        small = lax.dynamic_slice(blocks, (0, 1 - which, BIG * which, 0), (pairs, 1, SMALL, tokens))
        return jnp.concatenate([big.reshape(pairs * BIG, tokens), small.reshape(pairs * SMALL, tokens)])

    passed = lax.ppermute(half_of(1 - part), "xl", swap)
    mine = half_of(part)

    grads = out_grads[0, 0].reshape(2, rings, 3, size, tokens)

    def shifted(shift):
        heads = lax.dynamic_index_in_dim(grads, lax.rem(ring + shift, rings), 1, keepdims=False)
        return lax.ppermute(heads, "y", [(i, (i + shift) % rings) for i in range(rings)]) if shift else heads

    shifts = (0, 4, 3, 5, 2, 6, 1, 7)
    pieces = [shifted(shift) for shift in shifts]
    x = lax.all_gather(jnp.stack([mine, passed]), "y")
    x = x.reshape(augs, pairs * (BIG + SMALL), tokens)
    pieces = pieces[1:] + [lax.ppermute(piece, "xl", swap) for piece in pieces]
    y = call(
        functools.partial(prepare_kernel, shifts=shifts),
        jax.ShapeDtypeStruct((3, augs * tokens, 2 * LANES), jnp.bfloat16),
        [smem] + [vmem] * augs,
        name="prepare",
    )(jnp.stack([part, ring, aug_count[0]]), grads, *pieces)

    group = 2 * augs
    share, square = call(
        multiply_kernel,
        [
            jax.ShapeDtypeStruct((2, pairs, 3, 2, BIG, LANES), jnp.float32),
            jax.ShapeDtypeStruct((group, LANES), jnp.float32),
        ],
        [smem, hbm, hbm],
        out_specs=[vmem, vmem],
        scratch_shapes=[
            pltpu.VMEM(x.shape, x.dtype),
            pltpu.VMEM(y.shape, y.dtype),
            pltpu.SemaphoreType.DMA((4,)),
            pltpu.SemaphoreType.DMA((3,)),
        ],
        limit=MOST_VMEM,
        name="multiply",
    )(jnp.stack([part, core, aug_count[0]]), x, y)

    norms = lax.all_to_all(square, ("core", "xl", "y"), 0, 0, tiled=True)
    got = lax.ppermute(share, "core", swap)
    half = (1, pairs, 3, 2, BIG, LANES)
    pieces = call(
        functools.partial(clip_kernel, clip=clip, size=size),
        jax.ShapeDtypeStruct((3, pairs, 2, SMALL, LANES), jnp.int16),
        [
            smem,
            pl.BlockSpec((group, LANES), lambda i: (0, 0)),
            pl.BlockSpec(half, lambda i: (0, 0, 0, 0, 0, 0)),
            pl.BlockSpec(half, lambda i: (1, 0, 0, 0, 0, 0)),
        ],
        grid=(1,),
        out_specs=pl.BlockSpec((3, pairs, 2, SMALL, LANES), lambda i: (0, 0, 0, 0, 0)),
        name="clip",
    )(core.reshape(1), norms, share, got)

    pieces = pieces.reshape(2 * chips, SMALL, LANES)
    pieces = lax.all_to_all(pieces, ("z", "xh", "xl"), 0, 0, tiled=True)
    state = jax.ShapeDtypeStruct(noise.shape, jnp.float32)
    return call(
        functools.partial(update_kernel, weight=sigma * clip, images=float(images)),
        [state, state, state],
        [smem] + [vmem] * 4,
        out_specs=[vmem] * 3,
        name="update",
    )(core.reshape(1), pieces.reshape(chips, 2, SMALL, LANES), noise, first_moment, second_moment)


def solution(mesh):
    images, augs = mesh.devices.shape
    split = Mesh(mesh.devices.reshape(images // 4, 2, 2, 2, augs // 2), ("z", "xh", "core", "xl", "y"))
    dp, aug = ("z", "xh", "core"), ("xl", "y")
    state = P(dp, aug)
    run = jax.shard_map(
        body,
        mesh=split,
        in_specs=(P(dp, aug, None, None), P(dp, aug, None, None, None), P(dp), state, state, state),
        out_specs=(state, state, state),
        check_vma=False,
    )
    return lambda *args: tuple(run(*args))
```

```python
import functools
import math

import jax
import jax.numpy as jnp
from jax import lax
from jax.experimental import pallas as pl
from jax.experimental.pallas import tpu as pltpu
from jax.sharding import Mesh
from jax.sharding import PartitionSpec as P

LANES = 128
TOP = 32767.0
VMEM = 48 * 1024 * 1024
LESS_VMEM = 32 * 1024 * 1024
BIG, SMALL = 56, 48
SPARE = 24


def prepare_kernel(place, grads_ref, out_ref):
    part, ring, count = place[0], place[1], place[2]
    rings = grads_ref.shape[0] // 2
    size = grads_ref.shape[2]
    for j in range(3):
        out_ref[j, :, size:] = jnp.zeros((out_ref.shape[1], LANES - size), out_ref.dtype)
    for s in range(rings):
        for row in range(2):
            aug = jnp.bitwise_xor(part, row) * rings + lax.rem(ring - s + rings, rings)
            live = (aug < count).astype(jnp.float32).astype(jnp.bfloat16)
            at = (2 * s + row) * LANES
            for j in range(3):
                out_ref[j, at : at + LANES, :size] = (grads_ref[aug, j] * live).T


def multiply_kernel(place, *refs):
    *x_refs, own_ref, other_ref, out_ref, sum_ref = refs
    part, core, count = place[0], place[1], place[2]
    blocks = out_ref.shape[1] // 2
    slabs = [(ref, row) for ref in x_refs[:-2] for row in range(2)]
    slabs = slabs[:8] + [(ref, None) for ref in x_refs[-2:]] + slabs[8:]
    tiles = []
    at = 0
    for span in (BIG, SMALL):
        for i in range(2):
            tiles.append((at, span, i * blocks))
            at += blocks * span
    scale = 1.0 / count.astype(jnp.float32)
    big_slot = (part != core).astype(jnp.int32)
    squares = jnp.zeros((8, LANES), jnp.float32)
    for j in range(3):
        y = jnp.concatenate([own_ref[j], other_ref[j]], axis=1)
        for row, span, first in tiles:
            rows = blocks * span
            window = slice(row, row + rows)
            x = jnp.concatenate([ref[window] if k is None else ref[k, window] for ref, k in slabs], axis=1)
            slot = big_slot if span == BIG else 1 - big_slot
            acc = jnp.dot(x, y, preferred_element_type=jnp.float32) * scale
            square = jnp.sum((acc * acc).reshape(rows // 8, 8, 2 * LANES), axis=0)
            squares += square[:, :LANES] + square[:, LANES:]
            for b in range(blocks):
                for h in range(2):
                    out_ref[slot, first + b, j, h, :span] = acc[b * span : (b + 1) * span, h * LANES : (h + 1) * LANES]
                    if span < BIG:
                        out_ref[slot, first + b, j, h, span:] = jnp.zeros((BIG - span, LANES), jnp.float32)
    sum_ref[...] = jnp.broadcast_to(jnp.sum(squares, keepdims=True), sum_ref.shape)


def clip_kernel(place, norms_ref, keep_ref, got_ref, out_ref, *, clip, size):
    part, core = place[0], place[1]
    half = norms_ref.shape[0] // 2
    factors = []
    for c in range(2):
        total = jnp.sum(norms_ref[c * half : (c + 1) * half], axis=0, keepdims=True)
        factors.append(jnp.minimum(1.0, clip / jnp.sqrt(total + 1e-06)))
    mine = jnp.where(core == 0, factors[0], factors[1])
    theirs = jnp.where(core == 0, factors[1], factors[0])
    lane = lax.broadcasted_iota(jnp.int32, (8, LANES), 1)

    def block(k, carry):
        for j in range(3):
            for h in range(2):
                value = keep_ref[0, k, j, h] * mine + got_ref[0, k, j, h] * theirs
                top = jnp.maximum(jnp.max(jnp.abs(value), axis=1, keepdims=True), 1e-30)
                code = jnp.ceil(jnp.log2(top) * 8.0 + 0.05)
                value = jnp.round(value * (jnp.exp2(code * -0.125) * TOP))
                pieces = []
                for g in range(SMALL // 8):
                    if g < 5:
                        spare = pltpu.roll(value[SMALL:], (size - SPARE * g) % LANES, 1)
                    else:
                        spare = jnp.zeros((8, LANES), jnp.float32)
                        for q in range(BIG // 8):
                            spare = jnp.where(lane == size + q, code[8 * q : 8 * q + 8], spare)
                    pieces.append(jnp.where(lane < size, value[8 * g : 8 * g + 8], spare))
                piece = jnp.concatenate(pieces, axis=0)
                out_ref[j, k, jnp.bitwise_xor(part, h)] = piece.astype(jnp.int32).astype(jnp.int16)
        return carry

    lax.fori_loop(0, keep_ref.shape[1], block, 0)


def update_kernel(place, got_ref, noise_ref, first_ref, second_ref, grad_ref, new_first_ref, new_second_ref, *, weight, images):
    size = noise_ref.shape[1]
    lane = lax.broadcasted_iota(jnp.int32, (8, LANES), 1)
    zero = jnp.zeros((8, LANES), jnp.float32)
    halves = []
    for part in range(2):
        total = [zero] * (SMALL // 8)
        tails = [zero] * 5
        for k in range(got_ref.shape[0]):
            value = got_ref[k, part].astype(jnp.int32).astype(jnp.float32)
            scale = jnp.exp2(value[SMALL - 8 :] * 0.125) * (1.0 / TOP)
            for g in range(SMALL // 8):
                total[g] += value[8 * g : 8 * g + 8] * scale[:, size + g : size + g + 1]
            for g in range(5):
                tails[g] += value[8 * g : 8 * g + 8] * scale[:, size + 6 : size + 7]
        tail = zero
        for g in range(5):
            back = pltpu.roll(tails[g], (SPARE * g - size) % LANES, 1)
            tail = jnp.where((lane >= SPARE * g) & (lane < SPARE * (g + 1)), back, tail)
        halves.append(total + [tail])
    even = halves[0] + halves[1][:-1]
    odd = halves[0][:-1] + halves[1]
    total = jnp.concatenate([jnp.where(place[0] == 0, a, b) for a, b in zip(even, odd)], axis=0)[:, :size]
    grad = (total + weight * noise_ref[...]) / images
    grad_ref[...] = grad
    new_first_ref[...] = 0.9 * first_ref[...] + 0.1 * grad
    new_second_ref[...] = 0.999 * second_ref[...] + 0.001 * grad * grad


def call(kernel, out_shape, in_specs, limit=VMEM, **kw):
    return pl.pallas_call(
        kernel,
        in_specs=in_specs,
        out_shape=out_shape,
        compiler_params=pltpu.CompilerParams(vmem_limit_bytes=limit),
        **kw,
    )


def body(acts, out_grads, aug_count, noise, first_moment, second_moment):
    part, core, ring = lax.axis_index("xl"), lax.axis_index("core"), lax.axis_index("y")
    rings = lax.axis_size("y")
    augs = 2 * rings
    chips = lax.axis_size("z") * lax.axis_size("xh")
    images = 2 * chips
    width, tokens = acts.shape[2:]
    size = out_grads.shape[3] // 3
    pairs = width // size // 2
    clip = 0.5 * width * math.sqrt(3.0 * tokens / augs)
    sigma = 0.2 * math.sqrt(images) / width
    smem = pl.BlockSpec(memory_space=pltpu.SMEM)
    vmem = pl.BlockSpec(memory_space=pltpu.VMEM)
    swap = [(0, 1), (1, 0)]

    blocks = acts[0, 0].reshape(pairs, 2, size, tokens)

    def half_of(which):
        big = lax.dynamic_slice(blocks, (0, which, (size - BIG) * which, 0), (pairs, 1, BIG, tokens))
        small = lax.dynamic_slice(blocks, (0, 1 - which, BIG * which, 0), (pairs, 1, SMALL, tokens))
        return jnp.concatenate([big.reshape(pairs * BIG, tokens), small.reshape(pairs * SMALL, tokens)])

    passed = lax.ppermute(half_of(1 - part), "xl", swap)
    mine = half_of(part)

    block = jnp.stack([mine, passed])
    up = [(i, (i + 1) % rings) for i in range(rings)]
    down = [(i, (i - 1) % rings) for i in range(rings)]
    back, ahead = [block], [block]
    for _ in range(rings // 2 - 1):
        back.append(lax.ppermute(back[-1], "y", up))
        ahead.append(lax.ppermute(ahead[-1], "y", down))
    x = back + ahead[:0:-1] + [lax.ppermute(back[-1][0], "y", up), lax.ppermute(ahead[-1][1], "y", down)]

    grads = out_grads[0, 0].reshape(augs, 3, size, tokens)
    own = lax.all_to_all(grads, ("xl", "y"), 0, 0, tiled=True)
    other = lax.ppermute(own, "xl", swap)
    y = [
        call(
            prepare_kernel,
            jax.ShapeDtypeStruct((3, augs * tokens, LANES), jnp.bfloat16),
            [smem, vmem],
            limit=LESS_VMEM,
            name="prepare",
        )(jnp.stack([part, ring, aug_count[0]]), g)
        for g in (own, other)
    ]

    group = 2 * augs
    share, square = call(
        multiply_kernel,
        [
            jax.ShapeDtypeStruct((2, pairs, 3, 2, BIG, LANES), jnp.float32),
            jax.ShapeDtypeStruct((group, LANES), jnp.float32),
        ],
        [smem] + [vmem] * (len(x) + 2),
        out_specs=[vmem, vmem],
        limit=LESS_VMEM,
        name="multiply",
    )(jnp.stack([part, core, aug_count[0]]), *x, *y)

    norms = lax.all_to_all(square, ("core", "xl", "y"), 0, 0, tiled=True)
    got = lax.ppermute(share, "core", swap)
    half = (1, pairs, 3, 2, BIG, LANES)
    pieces = call(
        functools.partial(clip_kernel, clip=clip, size=size),
        jax.ShapeDtypeStruct((3, pairs, 2, SMALL, LANES), jnp.int16),
        [
            smem,
            pl.BlockSpec((group, LANES), lambda i: (0, 0)),
            pl.BlockSpec(half, lambda i: (0, 0, 0, 0, 0, 0)),
            pl.BlockSpec(half, lambda i: (1, 0, 0, 0, 0, 0)),
        ],
        grid=(1,),
        out_specs=pl.BlockSpec((3, pairs, 2, SMALL, LANES), lambda i: (0, 0, 0, 0, 0)),
        name="clip",
    )(jnp.stack([part, core]), norms, share, got)

    pieces = pieces.reshape(2 * chips, SMALL, LANES)
    pieces = lax.all_to_all(pieces, ("z", "xh", "xl"), 0, 0, tiled=True)
    state = jax.ShapeDtypeStruct(noise.shape, jnp.float32)
    return call(
        functools.partial(update_kernel, weight=sigma * clip, images=float(images)),
        [state, state, state],
        [smem] + [vmem] * 4,
        out_specs=[vmem] * 3,
        name="update",
    )(core.reshape(1), pieces.reshape(chips, 2, SMALL, LANES), noise, first_moment, second_moment)


def solution(mesh):
    images, augs = mesh.devices.shape
    split = Mesh(mesh.devices.reshape(images // 4, 2, 2, 2, augs // 2), ("z", "xh", "core", "xl", "y"))
    dp, aug = ("z", "xh", "core"), ("xl", "y")
    state = P(dp, aug)
    run = jax.shard_map(
        body,
        mesh=split,
        in_specs=(P(dp, aug, None, None), P(dp, aug, None, None, None), P(dp), state, state, state),
        out_specs=(state, state, state),
        check_vma=False,
    )
    return lambda *args: tuple(run(*args))
```

```python
import functools
import math

import jax
import jax.numpy as jnp
from jax import lax
from jax.experimental import pallas as pl
from jax.experimental.pallas import tpu as pltpu
from jax.sharding import Mesh
from jax.sharding import PartitionSpec as P

LANES = 128
TOP = 32767.0
VMEM = 48 * 1024 * 1024
LESS_VMEM = 32 * 1024 * 1024
BIG, SMALL = 56, 48
SPARE = 24


def prepare_kernel(place, grads_ref, out_ref):
    part, ring, count = place[0], place[1], place[2]
    rings = grads_ref.shape[0] // 2
    size = grads_ref.shape[2]
    for j in range(3):
        out_ref[j, :, size:] = jnp.zeros((out_ref.shape[1], LANES - size), out_ref.dtype)
    for s in range(rings):
        for row in range(2):
            aug = jnp.bitwise_xor(part, row) * rings + lax.rem(ring - s + rings, rings)
            live = (aug < count).astype(jnp.float32).astype(jnp.bfloat16)
            at = (2 * s + row) * LANES
            for j in range(3):
                out_ref[j, at : at + LANES, :size] = (grads_ref[aug, j] * live).T


def multiply_kernel(place, *refs):
    *x_refs, own_ref, other_ref, out_ref, sum_ref = refs
    part, core, count = place[0], place[1], place[2]
    blocks = out_ref.shape[1] // 2
    slabs = [(ref, row) for ref in x_refs for row in range(2)]
    tiles = []
    at = 0
    for span in (BIG, SMALL):
        for i in range(2):
            tiles.append((at, span, i * blocks))
            at += blocks * span
    scale = 1.0 / count.astype(jnp.float32)
    big_slot = (part != core).astype(jnp.int32)
    squares = jnp.zeros((8, LANES), jnp.float32)
    for j in range(3):
        y = jnp.concatenate([own_ref[j], other_ref[j]], axis=1)
        for row, span, first in tiles:
            rows = blocks * span
            window = slice(row, row + rows)
            x = jnp.concatenate([ref[k, window] for ref, k in slabs], axis=1)
            slot = big_slot if span == BIG else 1 - big_slot
            acc = jnp.dot(x, y, preferred_element_type=jnp.float32) * scale
            square = jnp.sum((acc * acc).reshape(rows // 8, 8, 2 * LANES), axis=0)
            squares += square[:, :LANES] + square[:, LANES:]
            for b in range(blocks):
                for h in range(2):
                    out_ref[slot, first + b, j, h, :span] = acc[b * span : (b + 1) * span, h * LANES : (h + 1) * LANES]
                    if span < BIG:
                        out_ref[slot, first + b, j, h, span:] = jnp.zeros((BIG - span, LANES), jnp.float32)
    sum_ref[...] = jnp.broadcast_to(jnp.sum(squares, keepdims=True), sum_ref.shape)


def clip_kernel(place, norms_ref, keep_ref, got_ref, out_ref, *, clip, size):
    part, core = place[0], place[1]
    half = norms_ref.shape[0] // 2
    factors = []
    for c in range(2):
        total = jnp.sum(norms_ref[c * half : (c + 1) * half], axis=0, keepdims=True)
        factors.append(jnp.minimum(1.0, clip / jnp.sqrt(total + 1e-06)))
    mine = jnp.where(core == 0, factors[0], factors[1])
    theirs = jnp.where(core == 0, factors[1], factors[0])
    lane = lax.broadcasted_iota(jnp.int32, (8, LANES), 1)

    def block(k, carry):
        for j in range(3):
            for h in range(2):
                value = keep_ref[0, k, j, h] * mine + got_ref[0, k, j, h] * theirs
                top = jnp.maximum(jnp.max(jnp.abs(value), axis=1, keepdims=True), 1e-30)
                code = jnp.ceil(jnp.log2(top) * 8.0 + 0.05)
                value = jnp.round(value * (jnp.exp2(code * -0.125) * TOP))
                pieces = []
                for g in range(SMALL // 8):
                    if g < 5:
                        spare = pltpu.roll(value[SMALL:], (size - SPARE * g) % LANES, 1)
                    else:
                        spare = jnp.zeros((8, LANES), jnp.float32)
                        for q in range(BIG // 8):
                            spare = jnp.where(lane == size + q, code[8 * q : 8 * q + 8], spare)
                    pieces.append(jnp.where(lane < size, value[8 * g : 8 * g + 8], spare))
                piece = jnp.concatenate(pieces, axis=0)
                out_ref[j, k, jnp.bitwise_xor(part, h)] = piece.astype(jnp.int32).astype(jnp.int16)
        return carry

    lax.fori_loop(0, keep_ref.shape[1], block, 0)


def update_kernel(place, got_ref, noise_ref, first_ref, second_ref, grad_ref, new_first_ref, new_second_ref, *, weight, images):
    size = noise_ref.shape[1]
    lane = lax.broadcasted_iota(jnp.int32, (8, LANES), 1)
    zero = jnp.zeros((8, LANES), jnp.float32)
    halves = []
    for part in range(2):
        total = [zero] * (SMALL // 8)
        tails = [zero] * 5
        for k in range(got_ref.shape[0]):
            value = got_ref[k, part].astype(jnp.int32).astype(jnp.float32)
            scale = jnp.exp2(value[SMALL - 8 :] * 0.125) * (1.0 / TOP)
            for g in range(SMALL // 8):
                total[g] += value[8 * g : 8 * g + 8] * scale[:, size + g : size + g + 1]
            for g in range(5):
                tails[g] += value[8 * g : 8 * g + 8] * scale[:, size + 6 : size + 7]
        tail = zero
        for g in range(5):
            back = pltpu.roll(tails[g], (SPARE * g - size) % LANES, 1)
            tail = jnp.where((lane >= SPARE * g) & (lane < SPARE * (g + 1)), back, tail)
        halves.append(total + [tail])
    even = halves[0] + halves[1][:-1]
    odd = halves[0][:-1] + halves[1]
    total = jnp.concatenate([jnp.where(place[0] == 0, a, b) for a, b in zip(even, odd)], axis=0)[:, :size]
    grad = (total + weight * noise_ref[...]) / images
    grad_ref[...] = grad
    new_first_ref[...] = 0.9 * first_ref[...] + 0.1 * grad
    new_second_ref[...] = 0.999 * second_ref[...] + 0.001 * grad * grad


def call(kernel, out_shape, in_specs, limit=VMEM, **kw):
    return pl.pallas_call(
        kernel,
        in_specs=in_specs,
        out_shape=out_shape,
        compiler_params=pltpu.CompilerParams(vmem_limit_bytes=limit),
        **kw,
    )


def body(acts, out_grads, aug_count, noise, first_moment, second_moment):
    part, core, ring = lax.axis_index("xl"), lax.axis_index("core"), lax.axis_index("y")
    rings = lax.axis_size("y")
    augs = 2 * rings
    chips = lax.axis_size("z") * lax.axis_size("xh")
    images = 2 * chips
    width, tokens = acts.shape[2:]
    size = out_grads.shape[3] // 3
    pairs = width // size // 2
    clip = 0.5 * width * math.sqrt(3.0 * tokens / augs)
    sigma = 0.2 * math.sqrt(images) / width
    smem = pl.BlockSpec(memory_space=pltpu.SMEM)
    vmem = pl.BlockSpec(memory_space=pltpu.VMEM)
    swap = [(0, 1), (1, 0)]

    blocks = acts[0, 0].reshape(pairs, 2, size, tokens)

    def half_of(which):
        big = lax.dynamic_slice(blocks, (0, which, (size - BIG) * which, 0), (pairs, 1, BIG, tokens))
        small = lax.dynamic_slice(blocks, (0, 1 - which, BIG * which, 0), (pairs, 1, SMALL, tokens))
        return jnp.concatenate([big.reshape(pairs * BIG, tokens), small.reshape(pairs * SMALL, tokens)])

    passed = lax.ppermute(half_of(1 - part), "xl", swap)
    mine = half_of(part)

    block = jnp.stack([mine, passed])
    up = [(i, (i + 1) % rings) for i in range(rings)]
    down = [(i, (i - 1) % rings) for i in range(rings)]
    back, ahead = [block], [block]
    for _ in range(rings // 2 - 1):
        back.append(lax.ppermute(back[-1], "y", up))
        ahead.append(lax.ppermute(ahead[-1], "y", down))
    back.append(lax.ppermute(back[-1], "y", up))
    x = back + ahead[:0:-1]

    grads = out_grads[0, 0].reshape(augs, 3, size, tokens)
    own = lax.all_to_all(grads, ("xl", "y"), 0, 0, tiled=True)
    other = lax.ppermute(own, "xl", swap)
    y = [
        call(
            prepare_kernel,
            jax.ShapeDtypeStruct((3, augs * tokens, LANES), jnp.bfloat16),
            [smem, vmem],
            limit=LESS_VMEM,
            name="prepare",
        )(jnp.stack([part, ring, aug_count[0]]), g)
        for g in (own, other)
    ]

    group = 2 * augs
    share, square = call(
        multiply_kernel,
        [
            jax.ShapeDtypeStruct((2, pairs, 3, 2, BIG, LANES), jnp.float32),
            jax.ShapeDtypeStruct((group, LANES), jnp.float32),
        ],
        [smem] + [vmem] * (len(x) + 2),
        out_specs=[vmem, vmem],
        limit=LESS_VMEM,
        name="multiply",
    )(jnp.stack([part, core, aug_count[0]]), *x, *y)

    norms = lax.all_to_all(square, ("core", "xl", "y"), 0, 0, tiled=True)
    got = lax.ppermute(share, "core", swap)
    half = (1, pairs, 3, 2, BIG, LANES)
    pieces = call(
        functools.partial(clip_kernel, clip=clip, size=size),
        jax.ShapeDtypeStruct((3, pairs, 2, SMALL, LANES), jnp.int16),
        [
            smem,
            pl.BlockSpec((group, LANES), lambda i: (0, 0)),
            pl.BlockSpec(half, lambda i: (0, 0, 0, 0, 0, 0)),
            pl.BlockSpec(half, lambda i: (1, 0, 0, 0, 0, 0)),
        ],
        grid=(1,),
        out_specs=pl.BlockSpec((3, pairs, 2, SMALL, LANES), lambda i: (0, 0, 0, 0, 0)),
        limit=LESS_VMEM,
        name="clip",
    )(jnp.stack([part, core]), norms, share, got)

    pieces = pieces.reshape(2 * chips, SMALL, LANES)
    pieces = lax.all_to_all(pieces, ("z", "xh", "xl"), 0, 0, tiled=True)
    state = jax.ShapeDtypeStruct(noise.shape, jnp.float32)
    return call(
        functools.partial(update_kernel, weight=sigma * clip, images=float(images)),
        [state, state, state],
        [smem] + [vmem] * 4,
        out_specs=[vmem] * 3,
        name="update",
    )(core.reshape(1), pieces.reshape(chips, 2, SMALL, LANES), noise, first_moment, second_moment)


def solution(mesh):
    images, augs = mesh.devices.shape
    split = Mesh(mesh.devices.reshape(images // 4, 2, 2, 2, augs // 2), ("z", "xh", "core", "xl", "y"))
    dp, aug = ("z", "xh", "core"), ("xl", "y")
    state = P(dp, aug)
    run = jax.shard_map(
        body,
        mesh=split,
        in_specs=(P(dp, aug, None, None), P(dp, aug, None, None, None), P(dp), state, state, state),
        out_specs=(state, state, state),
        check_vma=False,
    )
    return lambda *args: tuple(run(*args))
```

```python
import functools
import math

import jax
import jax.numpy as jnp
from jax import lax
from jax.experimental import pallas as pl
from jax.experimental.pallas import tpu as pltpu
from jax.sharding import Mesh
from jax.sharding import PartitionSpec as P

LANES = 128
TOP = 32767.0
VMEM = 48 * 1024 * 1024
LESS_VMEM = 32 * 1024 * 1024
BIG, SMALL = 56, 48
SPARE = 24


def prepare_kernel(place, grads_ref, out_ref):
    part, ring, count = place[0], place[1], place[2]
    rings = grads_ref.shape[0] // 2
    size = grads_ref.shape[2]
    for j in range(3):
        out_ref[j, :, size:] = jnp.zeros((out_ref.shape[1], LANES - size), out_ref.dtype)
    for s in range(rings):
        for row in range(2):
            aug = jnp.bitwise_xor(part, row) * rings + lax.rem(ring - s + rings, rings)
            live = (aug < count).astype(jnp.float32).astype(jnp.bfloat16)
            at = (2 * s + row) * LANES
            for j in range(3):
                out_ref[j, at : at + LANES, :size] = (grads_ref[aug, j] * live).T


def tiles_of(blocks):
    tiles = []
    at = 0
    for span in (BIG, SMALL):
        for i in range(2):
            tiles.append((at, span, i * blocks))
            at += blocks * span
    return tiles


def sum_kernel(*refs, near):
    *x_refs, own_ref, other_ref, out_ref = refs
    slabs = [(ref, k) for ref in x_refs for k in range(2)]
    tokens = x_refs[0].shape[2]
    for j in range(3):
        pieces = []
        for lo, hi in near:
            rows = slice(lo * tokens, hi * tokens)
            pieces.append(jnp.concatenate([own_ref[j, rows], other_ref[j, rows]], axis=1))
        y = jnp.concatenate(pieces, axis=0)
        for row, span, _ in tiles_of(x_refs[0].shape[1] // (2 * (BIG + SMALL))):
            window = slice(row, row + span * (x_refs[0].shape[1] // (2 * (BIG + SMALL))))
            x = jnp.concatenate([ref[k, window] for ref, k in slabs], axis=1)
            out_ref[j, window] = jnp.dot(x, y, preferred_element_type=jnp.float32)


def multiply_kernel(place, partial_ref, x_ref, own_ref, other_ref, out_ref, sum_ref, *, far):
    part, core, count = place[0], place[1], place[2]
    blocks = out_ref.shape[1] // 2
    tokens = x_ref.shape[2]
    scale = 1.0 / count.astype(jnp.float32)
    big_slot = (part != core).astype(jnp.int32)
    squares = jnp.zeros((8, LANES), jnp.float32)
    which = slice(far * tokens, (far + 2) * tokens)
    for j in range(3):
        y = jnp.concatenate([own_ref[j, which], other_ref[j, which]], axis=1)
        for row, span, first in tiles_of(blocks):
            rows = blocks * span
            window = slice(row, row + rows)
            x = jnp.concatenate([x_ref[0, window], x_ref[1, window]], axis=1)
            slot = big_slot if span == BIG else 1 - big_slot
            acc = (partial_ref[j, window] + jnp.dot(x, y, preferred_element_type=jnp.float32)) * scale
            square = jnp.sum((acc * acc).reshape(rows // 8, 8, 2 * LANES), axis=0)
            squares += square[:, :LANES] + square[:, LANES:]
            for b in range(blocks):
                for h in range(2):
                    out_ref[slot, first + b, j, h, :span] = acc[b * span : (b + 1) * span, h * LANES : (h + 1) * LANES]
                    if span < BIG:
                        out_ref[slot, first + b, j, h, span:] = jnp.zeros((BIG - span, LANES), jnp.float32)
    sum_ref[...] = jnp.broadcast_to(jnp.sum(squares, keepdims=True), sum_ref.shape)


def clip_kernel(place, norms_ref, keep_ref, got_hbm, out_ref, got_ref, sems, *, clip, size):
    part, core = place[0], place[1]
    step = got_ref.shape[0] // 4
    copies = []
    for q in range(4):
        some = pl.ds(q * step, step)
        copies.append(pltpu.make_async_copy(got_hbm.at[1, some], got_ref.at[some], sems.at[q]))
        copies[q].start()
    half = norms_ref.shape[0] // 2
    factors = []
    for c in range(2):
        total = jnp.sum(norms_ref[c * half : (c + 1) * half], axis=0, keepdims=True)
        factors.append(jnp.minimum(1.0, clip / jnp.sqrt(total + 1e-06)))
    mine = jnp.where(core == 0, factors[0], factors[1])
    theirs = jnp.where(core == 0, factors[1], factors[0])
    lane = lax.broadcasted_iota(jnp.int32, (8, LANES), 1)

    def block(k, carry):
        for j in range(3):
            for h in range(2):
                value = keep_ref[0, k, j, h] * mine + got_ref[k, j, h] * theirs
                top = jnp.maximum(jnp.max(jnp.abs(value), axis=1, keepdims=True), 1e-30)
                code = jnp.ceil(jnp.log2(top) * 8.0 + 0.05)
                value = jnp.round(value * (jnp.exp2(code * -0.125) * TOP))
                pieces = []
                for g in range(SMALL // 8):
                    if g < 5:
                        spare = pltpu.roll(value[SMALL:], (size - SPARE * g) % LANES, 1)
                    else:
                        spare = jnp.zeros((8, LANES), jnp.float32)
                        for q in range(BIG // 8):
                            spare = jnp.where(lane == size + q, code[8 * q : 8 * q + 8], spare)
                    pieces.append(jnp.where(lane < size, value[8 * g : 8 * g + 8], spare))
                piece = jnp.concatenate(pieces, axis=0)
                out_ref[j, k, jnp.bitwise_xor(part, h)] = piece.astype(jnp.int32).astype(jnp.int16)
        return carry

    for q in range(4):
        copies[q].wait()
        lax.fori_loop(q * step, (q + 1) * step, block, 0)


def update_kernel(place, got_ref, noise_ref, first_ref, second_ref, grad_ref, new_first_ref, new_second_ref, *, weight, images):
    size = noise_ref.shape[1]
    lane = lax.broadcasted_iota(jnp.int32, (8, LANES), 1)
    zero = jnp.zeros((8, LANES), jnp.float32)
    halves = []
    for part in range(2):
        total = [zero] * (SMALL // 8)
        tails = [zero] * 5
        for k in range(got_ref.shape[0]):
            value = got_ref[k, part].astype(jnp.int32).astype(jnp.float32)
            scale = jnp.exp2(value[SMALL - 8 :] * 0.125) * (1.0 / TOP)
            for g in range(SMALL // 8):
                total[g] += value[8 * g : 8 * g + 8] * scale[:, size + g : size + g + 1]
            for g in range(5):
                tails[g] += value[8 * g : 8 * g + 8] * scale[:, size + 6 : size + 7]
        tail = zero
        for g in range(5):
            back = pltpu.roll(tails[g], (SPARE * g - size) % LANES, 1)
            tail = jnp.where((lane >= SPARE * g) & (lane < SPARE * (g + 1)), back, tail)
        halves.append(total + [tail])
    even = halves[0] + halves[1][:-1]
    odd = halves[0][:-1] + halves[1]
    total = jnp.concatenate([jnp.where(place[0] == 0, a, b) for a, b in zip(even, odd)], axis=0)[:, :size]
    grad = (total + weight * noise_ref[...]) / images
    grad_ref[...] = grad
    new_first_ref[...] = 0.9 * first_ref[...] + 0.1 * grad
    new_second_ref[...] = 0.999 * second_ref[...] + 0.001 * grad * grad


def call(kernel, out_shape, in_specs, limit=VMEM, **kw):
    return pl.pallas_call(
        kernel,
        in_specs=in_specs,
        out_shape=out_shape,
        compiler_params=pltpu.CompilerParams(vmem_limit_bytes=limit),
        **kw,
    )


def body(acts, out_grads, aug_count, noise, first_moment, second_moment):
    part, core, ring = lax.axis_index("xl"), lax.axis_index("core"), lax.axis_index("y")
    rings = lax.axis_size("y")
    augs = 2 * rings
    chips = lax.axis_size("z") * lax.axis_size("xh")
    images = 2 * chips
    width, tokens = acts.shape[2:]
    size = out_grads.shape[3] // 3
    pairs = width // size // 2
    clip = 0.5 * width * math.sqrt(3.0 * tokens / augs)
    sigma = 0.2 * math.sqrt(images) / width
    smem = pl.BlockSpec(memory_space=pltpu.SMEM)
    vmem = pl.BlockSpec(memory_space=pltpu.VMEM)
    swap = [(0, 1), (1, 0)]

    blocks = acts[0, 0].reshape(pairs, 2, size, tokens)

    def half_of(which):
        big = lax.dynamic_slice(blocks, (0, which, (size - BIG) * which, 0), (pairs, 1, BIG, tokens))
        small = lax.dynamic_slice(blocks, (0, 1 - which, BIG * which, 0), (pairs, 1, SMALL, tokens))
        return jnp.concatenate([big.reshape(pairs * BIG, tokens), small.reshape(pairs * SMALL, tokens)])

    passed = lax.ppermute(half_of(1 - part), "xl", swap)
    mine = half_of(part)

    block = jnp.stack([mine, passed])
    up = [(i, (i + 1) % rings) for i in range(rings)]
    down = [(i, (i - 1) % rings) for i in range(rings)]
    back, ahead = [block], [block]
    for _ in range(rings // 2 - 1):
        back.append(lax.ppermute(back[-1], "y", up))
        ahead.append(lax.ppermute(ahead[-1], "y", down))
    back.append(lax.ppermute(back[-1], "y", up))
    x = back[:-1] + ahead[:0:-1]

    grads = out_grads[0, 0].reshape(augs, 3, size, tokens)
    own = lax.all_to_all(grads, ("xl", "y"), 0, 0, tiled=True)
    other = lax.ppermute(own, "xl", swap)
    y = [
        call(
            prepare_kernel,
            jax.ShapeDtypeStruct((3, augs * tokens, LANES), jnp.bfloat16),
            [smem, vmem],
            limit=LESS_VMEM,
            name="prepare",
        )(jnp.stack([part, ring, aug_count[0]]), g)
        for g in (own, other)
    ]

    rows = pairs * (BIG + SMALL)
    far = rings
    partial = call(
        functools.partial(sum_kernel, near=((0, far), (far + 2, augs))),
        jax.ShapeDtypeStruct((3, rows, 2 * LANES), jnp.float32),
        [vmem] * (len(x) + 2),
        limit=LESS_VMEM,
        cost_estimate=pl.CostEstimate(flops=12 * rows * LANES * (augs - 2) * tokens, bytes_accessed=1 << 23, transcendentals=0),
        name="sum",
    )(*x, *y)
    group = 2 * augs
    share, square = call(
        functools.partial(multiply_kernel, far=far),
        [
            jax.ShapeDtypeStruct((2, pairs, 3, 2, BIG, LANES), jnp.float32),
            jax.ShapeDtypeStruct((group, LANES), jnp.float32),
        ],
        [smem] + [vmem] * 4,
        out_specs=[vmem, vmem],
        limit=LESS_VMEM,
        name="multiply",
    )(jnp.stack([part, core, aug_count[0]]), partial, back[-1], *y)

    norms = lax.all_to_all(square, ("core", "xl", "y"), 0, 0, tiled=True)
    got = lax.ppermute(share, "core", swap)
    half = (1, pairs, 3, 2, BIG, LANES)
    pieces = call(
        functools.partial(clip_kernel, clip=clip, size=size),
        jax.ShapeDtypeStruct((3, pairs, 2, SMALL, LANES), jnp.int16),
        [
            smem,
            pl.BlockSpec((group, LANES), lambda i: (0, 0)),
            pl.BlockSpec(half, lambda i: (0, 0, 0, 0, 0, 0)),
            pl.BlockSpec(memory_space=pltpu.HBM),
        ],
        grid=(1,),
        out_specs=pl.BlockSpec((3, pairs, 2, SMALL, LANES), lambda i: (0, 0, 0, 0, 0)),
        scratch_shapes=[pltpu.VMEM(half[1:], jnp.float32), pltpu.SemaphoreType.DMA((4,))],
        limit=LESS_VMEM,
        name="clip",
    )(jnp.stack([part, core]), norms, share, got)

    pieces = pieces.reshape(2 * chips, SMALL, LANES)
    pieces = lax.all_to_all(pieces, ("z", "xh", "xl"), 0, 0, tiled=True)
    state = jax.ShapeDtypeStruct(noise.shape, jnp.float32)
    return call(
        functools.partial(update_kernel, weight=sigma * clip, images=float(images)),
        [state, state, state],
        [smem] + [vmem] * 4,
        out_specs=[vmem] * 3,
        name="update",
    )(core.reshape(1), pieces.reshape(chips, 2, SMALL, LANES), noise, first_moment, second_moment)


def solution(mesh):
    images, augs = mesh.devices.shape
    split = Mesh(mesh.devices.reshape(images // 4, 2, 2, 2, augs // 2), ("z", "xh", "core", "xl", "y"))
    dp, aug = ("z", "xh", "core"), ("xl", "y")
    state = P(dp, aug)
    run = jax.shard_map(
        body,
        mesh=split,
        in_specs=(P(dp, aug, None, None), P(dp, aug, None, None, None), P(dp), state, state, state),
        out_specs=(state, state, state),
        check_vma=False,
    )
    return lambda *args: tuple(run(*args))
```

```python
import functools
import math

import jax
import jax.numpy as jnp
from jax import lax
from jax.experimental import pallas as pl
from jax.experimental.pallas import tpu as pltpu
from jax.sharding import Mesh
from jax.sharding import PartitionSpec as P

LANES = 128
TOP = 32767.0
VMEM = 48 * 1024 * 1024
LESS_VMEM = 32 * 1024 * 1024
BIG, SMALL = 56, 48
SPARE = 24


def prepare_kernel(place, grads_ref, out_ref):
    part, ring, count = place[0], place[1], place[2]
    rings = grads_ref.shape[0] // 2
    size = grads_ref.shape[2]
    for j in range(3):
        out_ref[j, :, size:] = jnp.zeros((out_ref.shape[1], LANES - size), out_ref.dtype)
    for s in range(rings):
        for row in range(2):
            aug = jnp.bitwise_xor(part, row) * rings + lax.rem(ring - s + rings, rings)
            live = (aug < count).astype(jnp.float32).astype(jnp.bfloat16)
            at = (2 * s + row) * LANES
            for j in range(3):
                out_ref[j, at : at + LANES, :size] = (grads_ref[aug, j] * live).T


def tiles_of(blocks):
    tiles = []
    at = 0
    for span in (BIG, SMALL):
        for i in range(2):
            tiles.append((at, span, i * blocks))
            at += blocks * span
    return tiles


def sum_kernel(*refs, near):
    *x_refs, own_ref, other_ref, out_ref = refs
    slabs = [(ref, k) for ref in x_refs for k in range(2)]
    tokens = x_refs[0].shape[2]
    for j in range(3):
        pieces = []
        for lo, hi in near:
            rows = slice(lo * tokens, hi * tokens)
            pieces.append(jnp.concatenate([own_ref[j, rows], other_ref[j, rows]], axis=1))
        y = jnp.concatenate(pieces, axis=0)
        for row, span, _ in tiles_of(x_refs[0].shape[1] // (2 * (BIG + SMALL))):
            window = slice(row, row + span * (x_refs[0].shape[1] // (2 * (BIG + SMALL))))
            x = jnp.concatenate([ref[k, window] for ref, k in slabs], axis=1)
            out_ref[j, window] = jnp.dot(x, y, preferred_element_type=jnp.float32)


def multiply_kernel(place, partial_ref, x_ref, own_ref, other_ref, keep_ref, send_ref, sum_ref, *, far):
    part, core, count = place[0], place[1], place[2]
    blocks = keep_ref.shape[0] // 2
    tokens = x_ref.shape[2]
    scale = 1.0 / count.astype(jnp.float32)
    squares = jnp.zeros((8, LANES), jnp.float32)
    which = slice(far * tokens, (far + 2) * tokens)
    keeps_big = jnp.broadcast_to(part == core, (BIG, LANES))
    missing = jnp.zeros((BIG - SMALL, LANES), jnp.float32)
    tiles = tiles_of(blocks)
    for j in range(3):
        y = jnp.concatenate([own_ref[j, which], other_ref[j, which]], axis=1)
        for big, small in zip(tiles[:2], tiles[2:]):
            accs = []
            for row, span, first in (big, small):
                rows = blocks * span
                window = slice(row, row + rows)
                x = jnp.concatenate([x_ref[0, window], x_ref[1, window]], axis=1)
                acc = (partial_ref[j, window] + jnp.dot(x, y, preferred_element_type=jnp.float32)) * scale
                square = jnp.sum((acc * acc).reshape(rows // 8, 8, 2 * LANES), axis=0)
                squares += square[:, :LANES] + square[:, LANES:]
                accs.append(acc)
            for b in range(blocks):
                for h in range(2):
                    lanes = slice(h * LANES, (h + 1) * LANES)
                    more = accs[0][b * BIG : (b + 1) * BIG, lanes]
                    less = jnp.concatenate([accs[1][b * SMALL : (b + 1) * SMALL, lanes], missing], axis=0)
                    keep_ref[first + b, j, h] = jnp.where(keeps_big, more, less)
                    send_ref[first + b, j, h] = jnp.where(keeps_big, less, more)
    sum_ref[...] = jnp.broadcast_to(jnp.sum(squares, keepdims=True), sum_ref.shape)


def clip_kernel(place, norms_ref, keep_ref, got_ref, out_ref, *, clip, size):
    part, core = place[0], place[1]
    half = norms_ref.shape[0] // 2
    factors = []
    for c in range(2):
        total = jnp.sum(norms_ref[c * half : (c + 1) * half], axis=0, keepdims=True)
        factors.append(jnp.minimum(1.0, clip / jnp.sqrt(total + 1e-06)))
    mine = jnp.where(core == 0, factors[0], factors[1])
    theirs = jnp.where(core == 0, factors[1], factors[0])
    lane = lax.broadcasted_iota(jnp.int32, (8, LANES), 1)

    def run(flip):
        def block(k, carry):
            for j in range(3):
                for h in range(2):
                    value = keep_ref[k, j, h] * mine + got_ref[k, j, h] * theirs
                    top = jnp.maximum(jnp.max(jnp.abs(value), axis=1, keepdims=True), 1e-30)
                    code = jnp.ceil(jnp.log2(top) * 8.0 + 0.05)
                    value = jnp.round(value * (jnp.exp2(code * -0.125) * TOP))
                    pieces = []
                    for g in range(SMALL // 8):
                        if g < 5:
                            spare = pltpu.roll(value[SMALL:], (size - SPARE * g) % LANES, 1)
                        else:
                            spare = jnp.zeros((8, LANES), jnp.float32)
                            for q in range(BIG // 8):
                                spare = jnp.where(lane == size + q, code[8 * q : 8 * q + 8], spare)
                        pieces.append(jnp.where(lane < size, value[8 * g : 8 * g + 8], spare))
                    piece = jnp.concatenate(pieces, axis=0)
                    out_ref[j, k, h ^ flip] = piece.astype(jnp.int32).astype(jnp.int16)
            return carry

        lax.fori_loop(0, keep_ref.shape[0], block, 0)

    for flip in range(2):
        pl.when(part == flip)(functools.partial(run, flip))


def update_kernel(place, got_ref, noise_ref, first_ref, second_ref, grad_ref, new_first_ref, new_second_ref, *, weight, images):
    size = noise_ref.shape[1]
    lane = lax.broadcasted_iota(jnp.int32, (8, LANES), 1)
    zero = jnp.zeros((8, LANES), jnp.float32)
    halves = []
    for part in range(2):
        total = [zero] * (SMALL // 8)
        tails = [zero] * 5
        for k in range(got_ref.shape[0]):
            value = got_ref[k, part].astype(jnp.int32).astype(jnp.float32)
            scale = jnp.exp2(value[SMALL - 8 :] * 0.125) * (1.0 / TOP)
            for g in range(SMALL // 8):
                total[g] += value[8 * g : 8 * g + 8] * scale[:, size + g : size + g + 1]
            for g in range(5):
                tails[g] += value[8 * g : 8 * g + 8] * scale[:, size + 6 : size + 7]
        tail = zero
        for g in range(5):
            back = pltpu.roll(tails[g], (SPARE * g - size) % LANES, 1)
            tail = jnp.where((lane >= SPARE * g) & (lane < SPARE * (g + 1)), back, tail)
        halves.append(total + [tail])
    even = halves[0] + halves[1][:-1]
    odd = halves[0][:-1] + halves[1]
    total = jnp.concatenate([jnp.where(place[0] == 0, a, b) for a, b in zip(even, odd)], axis=0)[:, :size]
    grad = (total + weight * noise_ref[...]) / images
    grad_ref[...] = grad
    new_first_ref[...] = 0.9 * first_ref[...] + 0.1 * grad
    new_second_ref[...] = 0.999 * second_ref[...] + 0.001 * grad * grad


def call(kernel, out_shape, in_specs, limit=VMEM, **kw):
    return pl.pallas_call(
        kernel,
        in_specs=in_specs,
        out_shape=out_shape,
        compiler_params=pltpu.CompilerParams(vmem_limit_bytes=limit),
        **kw,
    )


def body(acts, out_grads, aug_count, noise, first_moment, second_moment):
    part, core, ring = lax.axis_index("xl"), lax.axis_index("core"), lax.axis_index("y")
    rings = lax.axis_size("y")
    augs = 2 * rings
    chips = lax.axis_size("z") * lax.axis_size("xh")
    images = 2 * chips
    width, tokens = acts.shape[2:]
    size = out_grads.shape[3] // 3
    pairs = width // size // 2
    clip = 0.5 * width * math.sqrt(3.0 * tokens / augs)
    sigma = 0.2 * math.sqrt(images) / width
    smem = pl.BlockSpec(memory_space=pltpu.SMEM)
    vmem = pl.BlockSpec(memory_space=pltpu.VMEM)
    swap = [(0, 1), (1, 0)]

    blocks = acts[0, 0].reshape(pairs, 2, size, tokens)

    def half_of(which):
        big = lax.dynamic_slice(blocks, (0, which, (size - BIG) * which, 0), (pairs, 1, BIG, tokens))
        small = lax.dynamic_slice(blocks, (0, 1 - which, BIG * which, 0), (pairs, 1, SMALL, tokens))
        return jnp.concatenate([big.reshape(pairs * BIG, tokens), small.reshape(pairs * SMALL, tokens)])

    passed = lax.ppermute(half_of(1 - part), "xl", swap)
    mine = half_of(part)

    block = jnp.stack([mine, passed])
    up = [(i, (i + 1) % rings) for i in range(rings)]
    down = [(i, (i - 1) % rings) for i in range(rings)]
    back, ahead = [block], [block]
    for _ in range(rings // 2 - 1):
        back.append(lax.ppermute(back[-1], "y", up))
        ahead.append(lax.ppermute(ahead[-1], "y", down))
    back.append(lax.ppermute(back[-1], "y", up))
    x = back[:-1] + ahead[:0:-1]

    grads = out_grads[0, 0].reshape(augs, 3, size, tokens)
    own = lax.all_to_all(grads, ("xl", "y"), 0, 0, tiled=True)
    other = lax.ppermute(own, "xl", swap)
    y = [
        call(
            prepare_kernel,
            jax.ShapeDtypeStruct((3, augs * tokens, LANES), jnp.bfloat16),
            [smem, vmem],
            limit=LESS_VMEM,
            name="prepare",
        )(jnp.stack([part, ring, aug_count[0]]), g)
        for g in (own, other)
    ]

    rows = pairs * (BIG + SMALL)
    far = rings
    partial = call(
        functools.partial(sum_kernel, near=((0, far), (far + 2, augs))),
        jax.ShapeDtypeStruct((3, rows, 2 * LANES), jnp.float32),
        [vmem] * (len(x) + 2),
        limit=LESS_VMEM,
        cost_estimate=pl.CostEstimate(flops=12 * rows * LANES * (augs - 2) * tokens, bytes_accessed=1 << 23, transcendentals=0),
        name="sum",
    )(*x, *y)
    group = 2 * augs
    half = jax.ShapeDtypeStruct((pairs, 3, 2, BIG, LANES), jnp.float32)
    keep, send, square = call(
        functools.partial(multiply_kernel, far=far),
        [half, half, jax.ShapeDtypeStruct((group, LANES), jnp.float32)],
        [smem] + [vmem] * 4,
        out_specs=[vmem] * 3,
        limit=LESS_VMEM,
        name="multiply",
    )(jnp.stack([part, core, aug_count[0]]), partial, back[-1], *y)

    norms = lax.all_to_all(square, ("core", "xl", "y"), 0, 0, tiled=True)
    got = lax.ppermute(send, "core", swap)
    pieces = call(
        functools.partial(clip_kernel, clip=clip, size=size),
        jax.ShapeDtypeStruct((3, pairs, 2, SMALL, LANES), jnp.int16),
        [smem] + [vmem] * 3,
        limit=LESS_VMEM,
        name="clip",
    )(jnp.stack([part, core]), norms, keep, got)

    pieces = pieces.reshape(2 * chips, SMALL, LANES)
    pieces = lax.all_to_all(pieces, ("z", "xh", "xl"), 0, 0, tiled=True)
    state = jax.ShapeDtypeStruct(noise.shape, jnp.float32)
    return call(
        functools.partial(update_kernel, weight=sigma * clip, images=float(images)),
        [state, state, state],
        [smem] + [vmem] * 4,
        out_specs=[vmem] * 3,
        name="update",
    )(core.reshape(1), pieces.reshape(chips, 2, SMALL, LANES), noise, first_moment, second_moment)


def solution(mesh):
    images, augs = mesh.devices.shape
    split = Mesh(mesh.devices.reshape(images // 4, 2, 2, 2, augs // 2), ("z", "xh", "core", "xl", "y"))
    dp, aug = ("z", "xh", "core"), ("xl", "y")
    state = P(dp, aug)
    run = jax.shard_map(
        body,
        mesh=split,
        in_specs=(P(dp, aug, None, None), P(dp, aug, None, None, None), P(dp), state, state, state),
        out_specs=(state, state, state),
        check_vma=False,
    )
    return lambda *args: tuple(run(*args))
```

```python
import functools
import math

import jax
import jax.numpy as jnp
from jax import lax
from jax.experimental import pallas as pl
from jax.experimental.pallas import tpu as pltpu
from jax.sharding import Mesh
from jax.sharding import PartitionSpec as P

LANES = 128
TOP = 32767.0
VMEM = 48 * 1024 * 1024
LESS_VMEM = 32 * 1024 * 1024
BIG, SMALL = 56, 48
SPARE = 24


def prepare_kernel(place, grads_ref, out_ref):
    part, ring, count = place[0], place[1], place[2]
    rings = grads_ref.shape[0] // 2
    size = grads_ref.shape[2]
    for j in range(3):
        out_ref[j, :, size:] = jnp.zeros((out_ref.shape[1], LANES - size), out_ref.dtype)
    for s in range(rings):
        for row in range(2):
            aug = jnp.bitwise_xor(part, row) * rings + lax.rem(ring - s + rings, rings)
            live = (aug < count).astype(jnp.float32).astype(jnp.bfloat16)
            at = (2 * s + row) * LANES
            for j in range(3):
                out_ref[j, at : at + LANES, :size] = (grads_ref[aug, j] * live).T


def tiles_of(blocks):
    tiles = []
    at = 0
    for span in (BIG, SMALL):
        for i in range(2):
            tiles.append((at, span, i * blocks))
            at += blocks * span
    return tiles


def sum_kernel(*refs, near):
    *x_refs, own_ref, other_ref, out_ref = refs
    slabs = [(ref, k) for ref in x_refs for k in range(2)]
    tokens = x_refs[0].shape[2]
    for j in range(3):
        pieces = []
        for lo, hi in near:
            rows = slice(lo * tokens, hi * tokens)
            pieces.append(jnp.concatenate([own_ref[j, rows], other_ref[j, rows]], axis=1))
        y = jnp.concatenate(pieces, axis=0)
        for row, span, _ in tiles_of(x_refs[0].shape[1] // (2 * (BIG + SMALL))):
            window = slice(row, row + span * (x_refs[0].shape[1] // (2 * (BIG + SMALL))))
            x = jnp.concatenate([ref[k, window] for ref, k in slabs], axis=1)
            out_ref[j, window] = jnp.dot(x, y, preferred_element_type=jnp.float32)


def multiply_kernel(place, partial_ref, x_ref, own_ref, other_ref, keep_ref, send_ref, sum_ref, *, far):
    part, core, count = place[0], place[1], place[2]
    blocks = keep_ref.shape[0] // 2
    tokens = x_ref.shape[2]
    scale = 1.0 / count.astype(jnp.float32)
    squares = jnp.zeros((8, LANES), jnp.float32)
    which = slice(far * tokens, (far + 2) * tokens)
    keeps_big = jnp.broadcast_to(part == core, (BIG, LANES))
    missing = jnp.zeros((BIG - SMALL, LANES), jnp.float32)
    tiles = tiles_of(blocks)
    for j in range(3):
        y = jnp.concatenate([own_ref[j, which], other_ref[j, which]], axis=1)
        for big, small in zip(tiles[:2], tiles[2:]):
            accs = []
            for row, span, first in (big, small):
                rows = blocks * span
                window = slice(row, row + rows)
                x = jnp.concatenate([x_ref[0, window], x_ref[1, window]], axis=1)
                acc = (partial_ref[j, window] + jnp.dot(x, y, preferred_element_type=jnp.float32)) * scale
                square = jnp.sum((acc * acc).reshape(rows // 8, 8, 2 * LANES), axis=0)
                squares += square[:, :LANES] + square[:, LANES:]
                accs.append(acc)
            for b in range(blocks):
                for h in range(2):
                    lanes = slice(h * LANES, (h + 1) * LANES)
                    more = accs[0][b * BIG : (b + 1) * BIG, lanes]
                    less = jnp.concatenate([accs[1][b * SMALL : (b + 1) * SMALL, lanes], missing], axis=0)
                    keep_ref[first + b, j, h] = jnp.where(keeps_big, more, less)
                    send_ref[first + b, j, h] = jnp.where(keeps_big, less, more)
    sum_ref[...] = jnp.broadcast_to(jnp.sum(squares, keepdims=True), sum_ref.shape)


def clip_kernel(place, norms_ref, keep_ref, got_ref, out_ref, *, clip, size):
    part, core = place[0], place[1]
    half = norms_ref.shape[0] // 2
    factors = []
    for c in range(2):
        total = jnp.sum(norms_ref[c * half : (c + 1) * half], axis=0, keepdims=True)
        factors.append(jnp.minimum(1.0, clip / jnp.sqrt(total + 1e-06)))
    mine = jnp.where(core == 0, factors[0], factors[1])
    theirs = jnp.where(core == 0, factors[1], factors[0])
    lane = lax.broadcasted_iota(jnp.int32, (8, LANES), 1)

    def run(flip):
        def block(k, carry):
            for j in range(3):
                for h in range(2):
                    value = keep_ref[k, j, h] * mine + got_ref[k, j, h] * theirs
                    top = jnp.maximum(jnp.max(jnp.abs(value), axis=1, keepdims=True), 1e-30)
                    code = jnp.ceil(jnp.log2(top) * 8.0 + 0.05)
                    value = jnp.round(value * (jnp.exp2(code * -0.125) * TOP))
                    pieces = []
                    for g in range(SMALL // 8):
                        if g < 5:
                            spare = pltpu.roll(value[SMALL:], (size - SPARE * g) % LANES, 1)
                        else:
                            spare = jnp.zeros((8, LANES), jnp.float32)
                            for q in range(BIG // 8):
                                spare = jnp.where(lane == size + q, code[8 * q : 8 * q + 8], spare)
                        pieces.append(jnp.where(lane < size, value[8 * g : 8 * g + 8], spare))
                    piece = jnp.concatenate(pieces, axis=0)
                    out_ref[j, k, h ^ flip] = piece.astype(jnp.int32).astype(jnp.int16)
            return carry

        lax.fori_loop(0, keep_ref.shape[0], block, 0)

    for flip in range(2):
        pl.when(part == flip)(functools.partial(run, flip))


def update_kernel(place, got_ref, noise_ref, first_ref, second_ref, grad_ref, new_first_ref, new_second_ref, *, weight, images):
    size = noise_ref.shape[1]
    lane = lax.broadcasted_iota(jnp.int32, (8, LANES), 1)
    zero = jnp.zeros((8, LANES), jnp.float32)
    halves = []
    for part in range(2):
        total = [zero] * (SMALL // 8)
        tails = [zero] * 5
        for k in range(got_ref.shape[0]):
            value = got_ref[k, part].astype(jnp.int32).astype(jnp.float32)
            scale = jnp.exp2(value[SMALL - 8 :] * 0.125) * (1.0 / TOP)
            for g in range(SMALL // 8):
                total[g] += value[8 * g : 8 * g + 8] * scale[:, size + g : size + g + 1]
            for g in range(5):
                tails[g] += value[8 * g : 8 * g + 8] * scale[:, size + 6 : size + 7]
        tail = zero
        for g in range(5):
            back = pltpu.roll(tails[g], (SPARE * g - size) % LANES, 1)
            tail = jnp.where((lane >= SPARE * g) & (lane < SPARE * (g + 1)), back, tail)
        halves.append(total + [tail])
    even = halves[0] + halves[1][:-1]
    odd = halves[0][:-1] + halves[1]
    total = jnp.concatenate([jnp.where(place[0] == 0, a, b) for a, b in zip(even, odd)], axis=0)[:, :size]
    grad = (total + weight * noise_ref[...]) / images
    grad_ref[...] = grad
    new_first_ref[...] = 0.9 * first_ref[...] + 0.1 * grad
    new_second_ref[...] = 0.999 * second_ref[...] + 0.001 * grad * grad


def call(kernel, out_shape, in_specs, limit=VMEM, **kw):
    return pl.pallas_call(
        kernel,
        in_specs=in_specs,
        out_shape=out_shape,
        compiler_params=pltpu.CompilerParams(vmem_limit_bytes=limit),
        **kw,
    )


def body(acts, out_grads, aug_count, noise, first_moment, second_moment):
    part, core, ring = lax.axis_index("xl"), lax.axis_index("core"), lax.axis_index("y")
    rings = lax.axis_size("y")
    augs = 2 * rings
    chips = lax.axis_size("z") * lax.axis_size("xh")
    images = 2 * chips
    width, tokens = acts.shape[2:]
    size = out_grads.shape[3] // 3
    pairs = width // size // 2
    clip = 0.5 * width * math.sqrt(3.0 * tokens / augs)
    sigma = 0.2 * math.sqrt(images) / width
    smem = pl.BlockSpec(memory_space=pltpu.SMEM)
    vmem = pl.BlockSpec(memory_space=pltpu.VMEM)
    swap = [(0, 1), (1, 0)]

    blocks = acts[0, 0].reshape(pairs, 2, size, tokens)

    def half_of(which):
        big = lax.dynamic_slice(blocks, (0, which, (size - BIG) * which, 0), (pairs, 1, BIG, tokens))
        small = lax.dynamic_slice(blocks, (0, 1 - which, BIG * which, 0), (pairs, 1, SMALL, tokens))
        return jnp.concatenate([big.reshape(pairs * BIG, tokens), small.reshape(pairs * SMALL, tokens)])

    passed = lax.ppermute(half_of(1 - part), "xl", swap)
    mine = half_of(part)

    block = jnp.stack([mine, passed])
    up = [(i, (i + 1) % rings) for i in range(rings)]
    down = [(i, (i - 1) % rings) for i in range(rings)]
    back, ahead = [block], [block]
    for _ in range(rings // 2 - 1):
        back.append(lax.ppermute(back[-1], "y", up))
        ahead.append(lax.ppermute(ahead[-1], "y", down))
    back.append(lax.ppermute(back[-1], "y", up))
    x = back[:-1] + ahead[:0:-1]

    grads = out_grads[0, 0].reshape(augs, 3, size, tokens)
    own = lax.all_to_all(grads, ("xl", "y"), 0, 0, tiled=True)
    other = lax.ppermute(own, "xl", swap)
    y = [
        call(
            prepare_kernel,
            jax.ShapeDtypeStruct((3, augs * tokens, LANES), jnp.bfloat16),
            [smem, vmem],
            limit=LESS_VMEM,
            name="prepare",
        )(jnp.stack([part, ring, aug_count[0]]), g)
        for g in (own, other)
    ]

    rows = pairs * (BIG + SMALL)
    far = rings
    partial = call(
        functools.partial(sum_kernel, near=((0, far), (far + 2, augs))),
        jax.ShapeDtypeStruct((3, rows, 2 * LANES), jnp.float32),
        [vmem] * (len(x) + 2),
        limit=LESS_VMEM,
        name="sum",
    )(*x, *y)
    group = 2 * augs
    half = jax.ShapeDtypeStruct((pairs, 3, 2, BIG, LANES), jnp.float32)
    keep, send, square = call(
        functools.partial(multiply_kernel, far=far),
        [half, half, jax.ShapeDtypeStruct((group, LANES), jnp.float32)],
        [smem] + [vmem] * 4,
        out_specs=[vmem] * 3,
        limit=LESS_VMEM,
        name="multiply",
    )(jnp.stack([part, core, aug_count[0]]), partial, back[-1], *y)

    norms = lax.all_to_all(square, ("core", "xl", "y"), 0, 0, tiled=True)
    got = lax.ppermute(send, "core", swap)
    pieces = call(
        functools.partial(clip_kernel, clip=clip, size=size),
        jax.ShapeDtypeStruct((3, pairs, 2, SMALL, LANES), jnp.int16),
        [smem] + [vmem] * 3,
        limit=LESS_VMEM,
        name="clip",
    )(jnp.stack([part, core]), norms, keep, got)

    pieces = pieces.reshape(2 * chips, SMALL, LANES)
    pieces = lax.all_to_all(pieces, ("z", "xh", "xl"), 0, 0, tiled=True)
    state = jax.ShapeDtypeStruct(noise.shape, jnp.float32)
    return call(
        functools.partial(update_kernel, weight=sigma * clip, images=float(images)),
        [state, state, state],
        [smem] + [vmem] * 4,
        out_specs=[vmem] * 3,
        name="update",
    )(core.reshape(1), pieces.reshape(chips, 2, SMALL, LANES), noise, first_moment, second_moment)


def solution(mesh):
    images, augs = mesh.devices.shape
    split = Mesh(mesh.devices.reshape(images // 4, 2, 2, 2, augs // 2), ("z", "xh", "core", "xl", "y"))
    dp, aug = ("z", "xh", "core"), ("xl", "y")
    state = P(dp, aug)
    run = jax.shard_map(
        body,
        mesh=split,
        in_specs=(P(dp, aug, None, None), P(dp, aug, None, None, None), P(dp), state, state, state),
        out_specs=(state, state, state),
        check_vma=False,
    )
    return lambda *args: tuple(run(*args))
```
